32 devices in a mesh: grp: 2 (over y), slab: 4 (over z), dom: 2 (over x), shot: 2 (over core).
Axes of the slice: x: 2, y: 2, z: 4, core: 2. Of those that a mesh axis runs over, the one named last changes fastest.
Arguments:
- particles: float32 [32, 16, 8, 128], P(('grp', 'dom'), 'slab'), parts along dimension 0, may hold values from -1.5 to 1.5
- background: float32 [32, 8, 128], P(('grp', 'slab')), parts along dimension 0, may hold values from 0.02 to 0.08
- wave_prev: bfloat16 [32, 2, 16, 8, 128], P(('grp', 'dom'), 'shot', 'slab'), parts along dimension 0, may hold values from -6 to 6
- wave_now: bfloat16 [32, 2, 16, 8, 128], P(('grp', 'dom'), 'shot', 'slab'), parts along dimension 0, may hold values from -6 to 6
- adjoint_near: bfloat16 [32, 2, 16, 8, 128], P(('grp', 'dom'), 'shot', 'slab'), parts along dimension 0, may hold values from -6 to 6
- adjoint_far: bfloat16 [32, 2, 16, 8, 128], P(('grp', 'dom'), 'shot', 'slab'), parts along dimension 0, may hold values from -6 to 6
- sources: int32 [4], P(('grp', 'shot')), parts along dimension 0, may hold values from 0 to 16383
- wavelet: float32 [4, 2], P(('grp', 'shot')), parts along dimension 0, may hold values from -16 to 16
- receivers: int32 [4, 128], P(('grp', 'shot')), parts along dimension 0, may hold values from 0 to 16383
- observed: float32 [4, 2, 128], P(('grp', 'shot')), parts along dimension 0, may hold values from -12 to 12
Outputs:
- update: float32 [32, 16, 8, 128], P(('grp', 'dom'), 'slab'), parts along dimension 0
The draws below stay inside these ranges and needn't reach their ends.
There are 2 independent parts, one for each index of `grp`. The reference program is written for one: setup_inputs(seed, part) draws one part's arguments, and reference() takes and returns one part's arrays. A program takes and returns all parts, laid end to end along the dimension named above; each array names one. Nothing has to cross between parts.
Inputs may be any that keep to these rules, and one draw needn't show every extreme that they name: `sources`: the flat index (z * 8 + x) * 128 + y of each shot's source cell. `receivers`: flat indices of the receiver cells; cells may repeat.
All inputs are finite; a program needn't handle non-finite values.
Results may differ from the reference program's by a relative error of at most 0.0003.
Values sent between devices are 32-bit elements; how exact they have to be, the bound alone decides.
No kernel may reach another device: no remote copies, remote signals or barrier semaphores. Data moves between devices by JAX's collectives and lax.ppermute only.
A program may use at most 64 MiB of HBM per device.

```python
import math
import jax
import jax.numpy as jnp
from jax import lax

NX = 8
NY = 128
RECV = 128
P_SIZE = 16
SHOTS = 2
NZ = 16


def draw_particles(key, part):
    key = jax.random.fold_in(key, 7)
    key_scale, key_noise, key_common = jax.random.split(key, 3)
    depth_factor = 1.0 + 2.0 * jnp.arange(NZ, dtype=jnp.float32) / max(NZ - 1, 1)
    scales = jnp.exp(jax.random.uniform(key_scale, (P_SIZE, 1, 1, 1), jnp.float32, math.log(0.02), math.log(0.2)))
    noise = jnp.clip(jax.random.normal(key_noise, (P_SIZE, NZ, NX, NY), jnp.float32), -2.5, 2.5)
    common = 0.15 * jnp.clip(jax.random.normal(key_common, (1, NZ, NX, NY), jnp.float32), -2.5, 2.5)
    model = common + scales * depth_factor[None, :, None, None] * noise
    return jnp.clip(model, -1.5, 1.5)


def with_ends(drawn, own_key, smallest, top_value):
    longest = drawn.shape.index(max(drawn.shape))
    spots = []
    for shift in (0, 1):
        where = [jax.random.randint(jax.random.fold_in(own_key, axis), (), 0, length) for axis, length in enumerate(drawn.shape)]
        where[longest] = (where[longest] + shift) % drawn.shape[longest]
        spots.append(tuple(where))
    return drawn.at[spots[0]].set(smallest).at[spots[1]].set(top_value)


def steps_of(stream_key, shape, cuts, smallest, top_value):
    factor_of, own = 1.0, jax.random.fold_in(stream_key, 6)
    for position, shards_of in cuts:
        heights = jnp.exp(jax.random.uniform(jax.random.fold_in(own, position), (shards_of,), jnp.float32, smallest / len(cuts), top_value / len(cuts)))
        factor_of = factor_of * jnp.repeat(heights, shape[position] // shards_of).reshape([-1 if axis == position else 1 for axis in range(len(shape))])
    return factor_of


def normal_values(key, extent, width, bound, shards=(), kind=jnp.bfloat16):
    values = jax.random.normal(key, extent, jnp.float32) * width
    if len(shards) > 0:
        values = steps_of(key, extent, shards, -0.22, 0.18) * values
    return jnp.clip(values, min=-bound, max=bound).astype(kind)


def setup_inputs(seed: int = 0, part: int = 0) -> dict:
    streams_of = jax.random.split(jax.random.key(seed), 11)
    part_keys = jax.random.split(jax.random.fold_in(streams_of[10], part), 11)
    return {
        "particles": draw_particles(jax.random.fold_in(jax.random.fold_in(streams_of[10], part), 71), part),
        "background": jnp.clip(jnp.exp(math.log(0.08) - 1.3862944 * jax.random.uniform(part_keys[1], (NZ, NX, NY), jnp.float32) ** steps_of(part_keys[1], (NZ, NX, NY), ((0, 4),), -0.2, 0.2)), 0.02, 0.08),
        "wave_prev": normal_values(part_keys[2], (P_SIZE, SHOTS, NZ, NX, NY), 1.0, 6.0, ((0, 2), (1, 2), (2, 4))),
        "wave_now": normal_values(part_keys[3], (P_SIZE, SHOTS, NZ, NX, NY), 1.0, 6.0, ((0, 2), (1, 2), (2, 4))),
        "adjoint_near": normal_values(part_keys[4], (P_SIZE, SHOTS, NZ, NX, NY), 1.0, 6.0, ((0, 2), (1, 2), (2, 4))),
        "adjoint_far": normal_values(part_keys[5], (P_SIZE, SHOTS, NZ, NX, NY), 1.0, 6.0, ((0, 2), (1, 2), (2, 4))),
        "sources": jax.random.randint(part_keys[6], (SHOTS,), 0, NZ * NX * NY).astype(jnp.int32),
        "wavelet": normal_values(part_keys[7], (SHOTS, 2), 4.0, 16.0, ((0, 2),), jnp.float32),
        "receivers": with_ends(jax.random.randint(part_keys[8], (SHOTS, RECV), 0, NZ * NX * NY), jax.random.fold_in(part_keys[8], 1), 0, (NZ * NX * NY) - 1).astype(jnp.int32),
        "observed": normal_values(part_keys[9], (SHOTS, 2, RECV), 3.0, 12.0, ((0, 2),), jnp.float32),
    }


DATA_WEIGHT = 0.5
PRIOR_WEIGHT = 4.0
REPEL_WEIGHT = 4.0
STENCIL_WEIGHTS = (-205.0 / 72.0, 8.0 / 5.0, -1.0 / 5.0, 8.0 / 315.0, -1.0 / 560.0)


def laplace(padded, layers, row_count, column_count):
    def window(along_z, along_x, along_y):
        return padded[..., 4 + along_z:4 + along_z + layers, 4 + along_x:4 + along_x + row_count, 4 + along_y:4 + along_y + column_count]

    result = (3.0 * STENCIL_WEIGHTS[0]) * window(0, 0, 0)
    for offset in range(1, 5):
        beside = window(offset, 0, 0) + window(-offset, 0, 0) + window(0, offset, 0)
        beside = beside + window(0, -offset, 0) + window(0, 0, offset) + window(0, 0, -offset)
        result = result + STENCIL_WEIGHTS[offset] * beside
    return result


def laplace_full(field):
    widths = [(0, 0)] * (field.ndim - 3) + [(4, 4)] * 3
    return laplace(jnp.pad(field, widths), NZ, NX, NY)


def reference(particles, background, wave_prev, wave_now, adjoint_near, adjoint_far, sources, wavelet, receivers, observed):
    cells = NZ * NX * NY
    cell_index = jnp.arange(cells, dtype=jnp.int32).reshape(NZ, NX, NY)
    source_mask = (cell_index[None] == sources[:, None, None, None]).astype(jnp.float32)
    shot_rows = jnp.arange(SHOTS, dtype=jnp.int32)[:, None]

    def record(field, column):
        return field.reshape(SHOTS, cells)[shot_rows, receivers] - observed[:, column]

    def inject(misfit):
        placed = jnp.zeros((SHOTS, cells), jnp.float32).at[shot_rows, receivers].add(misfit)
        return placed.reshape(SHOTS, NZ, NX, NY)

    def per_particle(items):
        model, zero_state, one_state, near_state, far_state = items
        squared = background * jnp.exp(model)
        wave_zero = zero_state.astype(jnp.float32)
        wave_one = one_state.astype(jnp.float32)
        laplace_one = laplace_full(wave_one)
        wave_two = 2.0 * wave_one - wave_zero + squared * laplace_one + wavelet[:, 0, None, None, None] * source_mask
        laplace_two = laplace_full(wave_two)
        wave_three = 2.0 * wave_two - wave_one + squared * laplace_two + wavelet[:, 1, None, None, None] * source_mask
        misfit_two = record(wave_two, 0)
        misfit_three = record(wave_three, 1)
        adjoint_four = near_state.astype(jnp.float32)
        adjoint_five = far_state.astype(jnp.float32)
        adjoint_three = 2.0 * adjoint_four - adjoint_five + laplace_full(squared * adjoint_four) - inject(misfit_three)
        adjoint_two = 2.0 * adjoint_three - adjoint_four + laplace_full(squared * adjoint_three) - inject(misfit_two)
        correlation = jnp.sum(adjoint_two * laplace_one + adjoint_three * laplace_two, axis=0)
        return DATA_WEIGHT * squared * correlation - PRIOR_WEIGHT * model

    scores = lax.map(per_particle, (particles, wave_prev, wave_now, adjoint_near, adjoint_far))
    flat_models = particles.reshape(P_SIZE, cells)
    flat_scores = scores.reshape(P_SIZE, cells)
    gram_matrix = jnp.dot(flat_models, flat_models.T, precision=lax.Precision.HIGHEST, preferred_element_type=jnp.float32)
    diagonal = jnp.diagonal(gram_matrix)
    distance = diagonal[:, None] + diagonal[None, :] - 2.0 * gram_matrix
    kernel_width = jnp.sum(distance) / (P_SIZE * (P_SIZE - 1) * math.log(P_SIZE))
    kernel = jnp.exp(-distance / kernel_width)
    weight = jnp.sum(kernel, axis=1)
    pulled = jnp.dot(kernel, flat_scores, precision=lax.Precision.HIGHEST, preferred_element_type=jnp.float32)
    centred = jnp.dot(kernel, flat_models, precision=lax.Precision.HIGHEST, preferred_element_type=jnp.float32)
    update = (pulled + REPEL_WEIGHT * (flat_models * weight[:, None] - centred)) / weight[:, None]
    return update.reshape(P_SIZE, NZ, NX, NY)
```

```python
import functools
import math

import jax
import jax.numpy as jnp
from jax import lax
from jax.experimental import pallas as pl
from jax.experimental.pallas import tpu as pltpu
from jax.sharding import PartitionSpec as P

DATA_WEIGHT = 0.5
PRIOR_WEIGHT = 4.0
REPEL_WEIGHT = 4.0
STENCIL = (-205.0 / 72.0, 8.0 / 5.0, -1.0 / 5.0, 8.0 / 315.0, -1.0 / 560.0)
RADIUS = 4
F32 = jnp.float32
HIGHEST = lax.Precision.HIGHEST


def call(body, outs, *operands, flops=1 << 20):
    moved = sum(x.size * x.dtype.itemsize for x in operands)
    return pl.pallas_call(
        body,
        out_shape=[jax.ShapeDtypeStruct(s, F32) for s in outs],
        in_specs=[pl.BlockSpec(memory_space=pltpu.VMEM)] * len(operands),
        out_specs=[pl.BlockSpec(memory_space=pltpu.VMEM)] * len(outs),
        compiler_params=pltpu.CompilerParams(vmem_limit_bytes=24 << 20),
        cost_estimate=pl.CostEstimate(flops=flops, bytes_accessed=moved, transcendentals=0),
    )(*operands)


def plane_weights(rows, columns):
    x = lax.broadcasted_iota(jnp.int32, (rows, columns), 0)
    y = lax.broadcasted_iota(jnp.int32, (rows, columns), 1)
    found = []
    for axis, at, size in ((0, x, rows), (1, y, columns)):
        for shift in range(-RADIUS, RADIUS + 1):
            if shift:
                inside = (at + shift >= 0) & (at + shift < size)
                found.append((axis, (-shift) % size, jnp.where(inside, STENCIL[abs(shift)], 0.0)))
    return found


def inner_laplace(planes, weights):
    result = []
    for z, here in enumerate(planes):
        total = (3.0 * STENCIL[0]) * here
        for other, plane in enumerate(planes):
            if other != z and abs(other - z) <= RADIUS:
                total = total + STENCIL[abs(other - z)] * plane
        for axis, shift, weight in weights:
            total = total + weight * pltpu.roll(here, shift, axis)
        result.append(total)
    return result


def outer_laplace(below, above, z, layers):
    total = None
    for j in range(RADIUS):
        for plane, distance in ((below[j], z + RADIUS - j), (above[j], layers + j - z)):
            if distance <= RADIUS:
                term = STENCIL[distance] * plane
                total = term if total is None else total + term
    return total


def planes_of(block, rows):
    return [block[z * rows : (z + 1) * rows] for z in range(block.shape[0] // rows)]


def sides(place_ref, first, second, rows, p):
    turned = place_ref[1:2, :] > 0
    low_on = place_ref[2:3, :] > 0
    high_on = place_ref[3:4, :] > 0
    a, b = planes_of(first[p], rows), planes_of(second[p], rows)
    below = [jnp.where(low_on, jnp.where(turned, v, u), 0.0) for u, v in zip(a, b)]
    above = [jnp.where(high_on, jnp.where(turned, u, v), 0.0) for u, v in zip(a, b)]
    return below, above


def loop(count, body):
    def step(p, carry):
        body(p)
        return carry

    lax.fori_loop(0, count, step, 0)


def solution(mesh):
    slabs, doms = mesh.shape["slab"], mesh.shape["dom"]
    up = [(2 * z, 2 * z + 2) for z in range(slabs - 1)] + [(2 * slabs - 2, 2 * slabs - 1)]
    up += [(2 * z + 1, 2 * z - 1) for z in range(1, slabs)] + [(1, 0)]
    down = [(b, a) for a, b in up]

    def exchange(block):
        return lax.ppermute(block, ("slab", "shot"), up), lax.ppermute(block, ("slab", "shot"), down)

    def from_dom(block, distance):
        return lax.ppermute(block, "dom", [((i + distance) % doms, i) for i in range(doms)])

    def other_shot(block):
        return lax.ppermute(block, "shot", [(0, 1), (1, 0)])

    def slab_sum(block):
        if slabs & (slabs - 1):
            return lax.psum(block, "slab")
        step = 1
        while step < slabs:
            block = block + lax.ppermute(block, "slab", [(i, i ^ step) for i in range(slabs)])
            step *= 2
        return block

    def local(
        particles,
        background,
        wave_prev,
        wave_now,
        adjoint_near,
        adjoint_far,
        sources,
        wavelet,
        receivers,
        observed,
    ):
        count, layers, rows, columns = particles.shape
        depth = layers * rows
        total = count * doms
        stack = (count, depth, columns)
        models = particles.reshape(stack)
        ground = background.reshape(depth, columns)
        zero, one, near, far = (
            field.reshape(stack) for field in (wave_prev, wave_now, adjoint_near, adjoint_far)
        )
        slab, shot = lax.axis_index("slab"), lax.axis_index("shot")
        place = jnp.stack([slab * depth, shot, slab > 0, slab < slabs - 1]).astype(jnp.int32)
        place = jnp.broadcast_to(jnp.pad(place, (0, 4))[:, None], (8, columns))

        def widen(one_ref, out_ref):
            out_ref[...] = one_ref[...].astype(F32)

        (wave_one,) = call(widen, [stack], one)
        one_first, one_second = exchange(wave_one)

        def medium(models_ref, ground_ref, near_ref, squared_ref, moved_ref):
            def particle(p):
                squared = ground_ref[...] * jnp.exp(models_ref[p])
                squared_ref[p] = squared
                moved_ref[p] = squared * near_ref[p].astype(F32)

            loop(count, particle)

        squared, near_moved = call(medium, [stack, stack], models, ground, near)
        near_first, near_second = exchange(near_moved)
        others = [from_dom(models, k) for k in range(1, doms)]

        def inner(one_ref, moved_ref, one_out, moved_out):
            weights = plane_weights(rows, columns)

            def particle(p):
                for source, out in ((one_ref, one_out), (moved_ref, moved_out)):
                    for z, plane in enumerate(inner_laplace(planes_of(source[p], rows), weights)):
                        out[p, z * rows : (z + 1) * rows] = plane

            loop(count, particle)

        one_inner, near_inner = call(inner, [stack, stack], wave_one, near_moved)

        def maps(place_ref, source_ref, wavelet_ref, receiver_ref, observed_ref, out_ref):
            first_row = place_ref[0:1, :]
            cells = receiver_ref[...]
            row = lax.shift_right_logical(cells, columns.bit_length() - 1) - first_row
            column = cells & (columns - 1)
            hit_row = lax.broadcasted_iota(jnp.int32, (depth, cells.shape[1]), 0) == row
            hit_column = lax.broadcasted_iota(jnp.int32, (columns, cells.shape[1]), 0) == column
            left = jnp.concatenate(
                [jnp.where(hit_row, value, 0.0) for value in (1.0, observed_ref[0:1], observed_ref[1:2])], axis=0
            )
            out_ref[0 : 3 * depth] = lax.dot_general(
                left,
                jnp.where(hit_column, 1.0, 0.0),
                (((1,), (1,)), ((), ())),
                precision=HIGHEST,
                preferred_element_type=F32,
            )
            cell = (lax.broadcasted_iota(jnp.int32, (depth, columns), 0) + first_row) * columns
            cell = cell + lax.broadcasted_iota(jnp.int32, (depth, columns), 1)
            at_source = cell == source_ref[...]
            out_ref[3 * depth : 4 * depth] = jnp.where(at_source, wavelet_ref[:, 0:1], 0.0)
            out_ref[4 * depth : 5 * depth] = jnp.where(at_source, wavelet_ref[:, 1:2], 0.0)

        (spots,) = call(
            maps,
            [(5 * depth, columns)],
            place,
            sources.reshape(1, 1),
            wavelet,
            receivers,
            observed.reshape(2, -1),
        )

        def second(place_ref, spots_ref, first, other, inner_ref, one_ref, zero_ref, squared_ref, lap_out, wave_out):
            def particle(p):
                below, above = sides(place_ref, first, other, rows, p)
                before = zero_ref[p].astype(F32)
                for z in range(layers):
                    at = slice(z * rows, (z + 1) * rows)
                    lap = inner_ref[p, at] + outer_laplace(below, above, z, layers)
                    lap_out[p, at] = lap
                    source = spots_ref[3 * depth + z * rows : 3 * depth + (z + 1) * rows]
                    wave_out[p, at] = 2.0 * one_ref[p, at] - before[at] + squared_ref[p, at] * lap + source

            loop(count, particle)

        lap_one, wave_two = call(
            second, [stack, stack], place, spots, one_first, one_second, one_inner, wave_one, zero, squared
        )
        two_first, two_second = exchange(wave_two)

        def gram(*refs):
            *parts, out_ref = refs
            height = total * rows
            same = None
            for z in range(layers):
                at = slice(z * rows, (z + 1) * rows)
                side = jnp.concatenate([part[:, at].reshape(count * rows, columns) for part in parts], axis=0)
                product = lax.dot_general(
                    side, side, (((1,), (1,)), ((), ())), precision=HIGHEST, preferred_element_type=F32
                )
                same = product if same is None else same + product
            r = lax.broadcasted_iota(jnp.int32, (height, height), 0)
            c = lax.broadcasted_iota(jnp.int32, (height, height), 1)
            same = jnp.where(r % rows == c % rows, same, 0.0)
            pick = jnp.where(
                lax.broadcasted_iota(jnp.int32, (total, height), 1) // rows
                == lax.broadcasted_iota(jnp.int32, (total, height), 0),
                1.0,
                0.0,
            )
            half = jnp.dot(pick, same, precision=HIGHEST, preferred_element_type=F32)
            out_ref[...] = lax.dot_general(
                half, pick, (((1,), (1,)), ((), ())), precision=HIGHEST, preferred_element_type=F32
            )

        (partial_gram,) = call(gram, [(total, total)], models, *others)
        full_gram = slab_sum(partial_gram)

        def third_base(place_ref, first, other, inner_ref, near_ref, far_ref, two_ref, base_out, inner_out):
            weights = plane_weights(rows, columns)

            def particle(p):
                below, above = sides(place_ref, first, other, rows, p)
                later = 2.0 * near_ref[p].astype(F32) - far_ref[p].astype(F32)
                for z in range(layers):
                    at = slice(z * rows, (z + 1) * rows)
                    base_out[p, at] = later[at] + inner_ref[p, at] + outer_laplace(below, above, z, layers)
                for z, plane in enumerate(inner_laplace(planes_of(two_ref[p], rows), weights)):
                    inner_out[p, z * rows : (z + 1) * rows] = plane

            loop(count, particle)

        base, two_inner = call(
            third_base, [stack, stack], place, near_first, near_second, near_inner, near, far, wave_two
        )

        def third(
            place_ref, spots_ref, first, other, inner_ref, one_ref, two_ref, squared_ref, base_ref, lap_out, three_out, moved_out
        ):
            def particle(p):
                below, above = sides(place_ref, first, other, rows, p)
                for z in range(layers):
                    at = slice(z * rows, (z + 1) * rows)
                    hits, _, seen, _, source = (
                        spots_ref[k * depth + z * rows : k * depth + (z + 1) * rows] for k in range(5)
                    )
                    lap = inner_ref[p, at] + outer_laplace(below, above, z, layers)
                    lap_out[p, at] = lap
                    wave_three = 2.0 * two_ref[p, at] - one_ref[p, at] + squared_ref[p, at] * lap + source
                    three = base_ref[p, at] - (hits * wave_three - seen)
                    three_out[p, at] = three
                    moved_out[p, at] = squared_ref[p, at] * three

            loop(count, particle)

        lap_two, three, three_moved = call(
            third,
            [stack, stack, stack],
            place,
            spots,
            two_first,
            two_second,
            two_inner,
            wave_one,
            wave_two,
            squared,
            base,
        )
        three_first, three_second = exchange(three_moved)

        def fourth_base(spots_ref, moved_ref, three_ref, near_ref, two_ref, lap_one_ref, lap_two_ref, out_ref):
            weights = plane_weights(rows, columns)

            def particle(p):
                before = near_ref[p].astype(F32)
                for z, lap in enumerate(inner_laplace(planes_of(moved_ref[p], rows), weights)):
                    at = slice(z * rows, (z + 1) * rows)
                    hits = spots_ref[at]
                    seen = spots_ref[depth + z * rows : depth + (z + 1) * rows]
                    three = three_ref[p, at]
                    two = 2.0 * three - before[at] + lap - (hits * two_ref[p, at] - seen)
                    out_ref[p, at] = two * lap_one_ref[p, at] + three * lap_two_ref[p, at]

            loop(count, particle)

        (inner_correlation,) = call(
            fourth_base, [stack], spots, three_moved, three, near, wave_two, lap_one, lap_two
        )

        def fourth(place_ref, first, other, inner_ref, lap_one_ref, squared_ref, out_ref):
            def particle(p):
                below, above = sides(place_ref, first, other, rows, p)
                for z in range(layers):
                    at = slice(z * rows, (z + 1) * rows)
                    full = inner_ref[p, at] + outer_laplace(below, above, z, layers) * lap_one_ref[p, at]
                    out_ref[p, at] = DATA_WEIGHT * squared_ref[p, at] * full

            loop(count, particle)

        (pull,) = call(fourth, [stack], place, three_first, three_second, inner_correlation, lap_one, squared)
        pulls = [pull] + [from_dom(pull, k) for k in range(1, doms)]
        pulls = pulls + [other_shot(block) for block in pulls]

        def spread(gram_ref, out_ref):
            r = lax.broadcasted_iota(jnp.int32, (total, total), 0)
            c = lax.broadcasted_iota(jnp.int32, (total, total), 1)
            value = gram_ref[...]
            diagonal = jnp.where(r == c, value, 0.0)
            distance = jnp.sum(diagonal, axis=1, keepdims=True) + jnp.sum(diagonal, axis=0, keepdims=True) - 2.0 * value
            width = jnp.sum(jnp.sum(distance, axis=1, keepdims=True), axis=0, keepdims=True) / (
                total * (total - 1) * math.log(total)
            )
            kernel = jnp.exp(-distance / width)
            kernel = kernel / jnp.sum(kernel, axis=1, keepdims=True)
            tall, wide = count * rows, total * rows
            pick_row = jnp.where(
                lax.broadcasted_iota(jnp.int32, (tall, total), 0) // rows
                == lax.broadcasted_iota(jnp.int32, (tall, total), 1),
                1.0,
                0.0,
            )
            pick_column = jnp.where(
                lax.broadcasted_iota(jnp.int32, (total, wide), 1) // rows
                == lax.broadcasted_iota(jnp.int32, (total, wide), 0),
                1.0,
                0.0,
            )
            half = jnp.dot(pick_row, kernel, precision=HIGHEST, preferred_element_type=F32)
            full = jnp.dot(half, pick_column, precision=HIGHEST, preferred_element_type=F32)
            same = (
                lax.broadcasted_iota(jnp.int32, (tall, wide), 0) % rows
                == lax.broadcasted_iota(jnp.int32, (tall, wide), 1) % rows
            )
            out_ref[...] = jnp.where(same, full, 0.0)

        (spread_kernel,) = call(spread, [(count * rows, total * rows)], full_gram)

        def finish(kernel_ref, *refs):
            model_refs, pull_refs, out_ref = refs[:doms], refs[doms : 3 * doms], refs[3 * doms]
            for z in range(layers):
                at = slice(z * rows, (z + 1) * rows)
                side = jnp.concatenate(
                    [
                        (
                            pull_refs[k][:, at]
                            + pull_refs[doms + k][:, at]
                            - (PRIOR_WEIGHT + REPEL_WEIGHT) * model_refs[k][:, at]
                        ).reshape(count * rows, columns)
                        for k in range(doms)
                    ],
                    axis=0,
                )
                pulled = jnp.dot(kernel_ref[...], side, precision=HIGHEST, preferred_element_type=F32)
                out_ref[:, at] = pulled.reshape(count, rows, columns) + REPEL_WEIGHT * model_refs[0][:, at]

        (update,) = call(finish, [stack], spread_kernel, models, *others, *pulls)
        return update.reshape(particles.shape)

    placed = (
        P(("grp", "dom"), "slab", None, None),
        P(("grp", "slab"), None, None),
        P(("grp", "dom"), "shot", "slab", None, None),
        P(("grp", "dom"), "shot", "slab", None, None),
        P(("grp", "dom"), "shot", "slab", None, None),
        P(("grp", "dom"), "shot", "slab", None, None),
        P(("grp", "shot")),
        P(("grp", "shot"), None),
        P(("grp", "shot"), None),
        P(("grp", "shot"), None, None),
    )
    return jax.shard_map(
        local,
        mesh=mesh,
        in_specs=placed,
        out_specs=P(("grp", "dom"), "slab", None, None),
        check_vma=False,
    )
```

```python
import functools
import math

import jax
import jax.numpy as jnp
from jax import lax
from jax.experimental import pallas as pl
from jax.experimental.pallas import tpu as pltpu
from jax.sharding import PartitionSpec as P

DATA_WEIGHT = 0.5
PRIOR_WEIGHT = 4.0
REPEL_WEIGHT = 4.0
STENCIL = (-205.0 / 72.0, 8.0 / 5.0, -1.0 / 5.0, 8.0 / 315.0, -1.0 / 560.0)
RADIUS = 4
F32 = jnp.float32
HIGHEST = lax.Precision.HIGHEST


def call(body, outs, *operands, far=0, scratch=(), flops=1 << 20):
    moved = sum(x.size * x.dtype.itemsize for x in operands)
    outs = [x if isinstance(x, jax.ShapeDtypeStruct) else jax.ShapeDtypeStruct(x, F32) for x in outs]
    near = pl.BlockSpec(memory_space=pltpu.VMEM)
    operands = [pltpu.with_memory_space_constraint(x, pltpu.HBM) for x in operands[:far]] + list(operands[far:])
    return pl.pallas_call(
        body,
        out_shape=outs,
        in_specs=[pl.BlockSpec(memory_space=pltpu.HBM)] * far + [near] * (len(operands) - far),
        out_specs=[near] * len(outs),
        scratch_shapes=list(scratch),
        compiler_params=pltpu.CompilerParams(vmem_limit_bytes=24 << 20),
        cost_estimate=pl.CostEstimate(flops=flops, bytes_accessed=moved, transcendentals=0),
    )(*operands)


def fetch(sources, targets, semaphores):
    copies = [
        pltpu.make_async_copy(source, target, semaphores.at[k])
        for k, (source, target) in enumerate(zip(sources, targets))
    ]
    for copy in copies:
        copy.start()
    return copies


def plane_weights(rows, columns):
    x = lax.broadcasted_iota(jnp.int32, (rows, columns), 0)
    y = lax.broadcasted_iota(jnp.int32, (rows, columns), 1)
    found = []
    for axis, at, size in ((0, x, rows), (1, y, columns)):
        for shift in range(-RADIUS, RADIUS + 1):
            if shift:
                inside = (at + shift >= 0) & (at + shift < size)
                found.append((axis, (-shift) % size, jnp.where(inside, STENCIL[abs(shift)], 0.0)))
    return found


def inner_laplace(planes, weights):
    result = []
    for z, here in enumerate(planes):
        middle = (3.0 * STENCIL[0]) * here
        for other, plane in enumerate(planes):
            if other != z and abs(other - z) <= RADIUS:
                middle = middle + STENCIL[abs(other - z)] * plane
        parts = [middle]
        for low in range(0, len(weights), 4):
            some = None
            for axis, shift, weight in weights[low : low + 4]:
                term = weight * pltpu.roll(here, shift, axis)
                some = term if some is None else some + term
            parts.append(some)
        while len(parts) > 1:
            parts = [sum(parts[k : k + 2][1:], parts[k]) for k in range(0, len(parts), 2)]
        result.append(parts[0])
    return result


def outer_laplace(below, above, z, layers):
    total = None
    for j in range(RADIUS):
        for plane, distance in ((below[j], z + RADIUS - j), (above[j], layers + j - z)):
            if distance <= RADIUS:
                term = STENCIL[distance] * plane
                total = term if total is None else total + term
    return total


def planes_of(block, rows):
    return [block[z * rows : (z + 1) * rows] for z in range(block.shape[0] // rows)]


def side_masks(rows, columns):
    slab = jnp.full((rows, columns), lax.axis_index("slab"), jnp.int32)
    shot = jnp.full((rows, columns), lax.axis_index("shot"), jnp.int32)
    return shot > 0, slab > 0, slab < lax.axis_size("slab") - 1


def sides(masks, first, second, rows, p):
    turned, low_on, high_on = masks
    a, b = planes_of(first[p], rows), planes_of(second[p], rows)
    below = [jnp.where(low_on, jnp.where(turned, v, u), 0.0) for u, v in zip(a, b)]
    above = [jnp.where(high_on, jnp.where(turned, u, v), 0.0) for u, v in zip(a, b)]
    return below, above


def loop(count, body, together=2):
    if count % together:
        together = 1

    def step(group, carry):
        for p in range(together):
            body(group * together + p)
        return carry

    lax.fori_loop(0, count // together, step, 0)


def solution(mesh):
    slabs, doms = mesh.shape["slab"], mesh.shape["dom"]
    up = [(2 * z, 2 * z + 2) for z in range(slabs - 1)] + [(2 * slabs - 2, 2 * slabs - 1)]
    up += [(2 * z + 1, 2 * z - 1) for z in range(1, slabs)] + [(1, 0)]
    down = [(b, a) for a, b in up]

    def exchange(block):
        return lax.ppermute(block, ("slab", "shot"), up), lax.ppermute(block, ("slab", "shot"), down)

    def from_dom(block, distance):
        return lax.ppermute(block, "dom", [((i + distance) % doms, i) for i in range(doms)])

    def other_shot(block):
        return lax.ppermute(block, "shot", [(0, 1), (1, 0)])

    halving = slabs >= 4 and slabs & (slabs - 1) == 0

    def from_slab(block, step):
        if not halving:
            return jnp.zeros_like(block)
        return lax.ppermute(block, "slab", [(i, i ^ step) for i in range(slabs)])

    def local(
        particles,
        background,
        wave_prev,
        wave_now,
        adjoint_near,
        adjoint_far,
        sources,
        wavelet,
        receivers,
        observed,
    ):
        count, layers, rows, columns = particles.shape
        depth = layers * rows
        total = count * doms
        stack = (count, depth, columns)
        at_plane = [slice(z * rows, (z + 1) * rows) for z in range(layers)]
        models = particles.reshape(stack)
        ground = background.reshape(depth, columns)
        zero, one, near, far = (
            field.reshape(stack) for field in (wave_prev, wave_now, adjoint_near, adjoint_far)
        )

        halves = jax.ShapeDtypeStruct(stack, one.dtype)

        def prepare(one_hbm, models_hbm, ground_hbm, near_hbm, wave_ref, squared_ref, moved_ref, models_ref, near_ref, one_ref, ground_ref, arrived):
            copies = fetch(
                (one_hbm, models_hbm, ground_hbm, near_hbm), (one_ref, models_ref, ground_ref, near_ref), arrived
            )
            for copy in copies:
                copy.wait()

            def particle(p):
                wave_ref[p] = one_ref[p].astype(F32)
                squared = ground_ref[...] * jnp.exp(models_ref[p])
                squared_ref[p] = squared
                moved_ref[p] = squared * near_ref[p].astype(F32)

            loop(count, particle)

        wave_one, squared, near_moved, models, near = call(
            prepare,
            [stack] * 4 + [halves],
            one,
            models,
            ground,
            near,
            far=4,
            scratch=[
                pltpu.VMEM(stack, one.dtype),
                pltpu.VMEM((depth, columns), F32),
                pltpu.SemaphoreType.DMA((4,)),
            ],
        )
        one_first, one_second = exchange(wave_one)
        near_first, near_second = exchange(near_moved)
        others = [from_dom(models, k) for k in range(1, doms)]

        def first_base(*refs):
            far_away, (source_ref, one_ref, inner_out, spots_out), held = refs[:5], refs[5:9], refs[9:14]
            wavelet_ref, receiver_ref, observed_ref = held[2:]
            copies = fetch(far_away, held, refs[14])
            weights = plane_weights(rows, columns)

            def particle(p):
                for at, plane in zip(at_plane, inner_laplace(planes_of(one_ref[p], rows), weights)):
                    inner_out[p, at] = plane

            loop(count, particle)
            for copy in copies:
                copy.wait()
            first_row = lax.axis_index("slab") * depth
            cells = receiver_ref[...]
            row = lax.shift_right_logical(cells, columns.bit_length() - 1) - first_row
            column = cells & (columns - 1)
            hit_row = lax.broadcasted_iota(jnp.int32, (depth, cells.shape[1]), 0) == row
            hit_column = lax.broadcasted_iota(jnp.int32, (columns, cells.shape[1]), 0) == column
            left = jnp.concatenate(
                [jnp.where(hit_row, value, 0.0) for value in (1.0, observed_ref[0:1], observed_ref[1:2])], axis=0
            )
            spots_out[0 : 3 * depth] = lax.dot_general(
                left,
                jnp.where(hit_column, 1.0, 0.0),
                (((1,), (1,)), ((), ())),
                precision=HIGHEST,
                preferred_element_type=F32,
            )
            cell = (lax.broadcasted_iota(jnp.int32, (depth, columns), 0) + first_row) * columns
            cell = cell + lax.broadcasted_iota(jnp.int32, (depth, columns), 1)
            at_source = cell == source_ref[...]
            spots_out[3 * depth : 4 * depth] = jnp.where(at_source, wavelet_ref[:, 0:1], 0.0)
            spots_out[4 * depth : 5 * depth] = jnp.where(at_source, wavelet_ref[:, 1:2], 0.0)

        small = (wavelet, receivers, observed.reshape(2, -1))
        one_inner, spots, zero, far = call(
            first_base,
            [stack, (5 * depth, columns), halves, halves],
            zero,
            far,
            *small,
            sources.reshape(1, 1),
            wave_one,
            far=5,
            scratch=[pltpu.VMEM(x.shape, x.dtype) for x in small] + [pltpu.SemaphoreType.DMA((5,))],
        )

        def spot(spots_ref, kind, z):
            return spots_ref[kind * depth + z * rows : kind * depth + (z + 1) * rows]

        def first(spots_ref, first, second, inner_ref, one_ref, zero_ref, squared_ref, lap_out, wave_out):
            masks = side_masks(rows, columns)

            def particle(p):
                below, above = sides(masks, first, second, rows, p)
                before = zero_ref[p].astype(F32)
                for z, at in enumerate(at_plane):
                    lap = inner_ref[p, at] + outer_laplace(below, above, z, layers)
                    lap_out[p, at] = lap
                    moved = squared_ref[p, at] * lap + spot(spots_ref, 3, z)
                    wave_out[p, at] = 2.0 * one_ref[p, at] - before[at] + moved

            loop(count, particle)

        lap_one, wave_two = call(
            first, [stack] * 2, spots, one_first, one_second, one_inner, wave_one, zero, squared
        )
        two_first, two_second = exchange(wave_two)

        def gram(*refs):
            *parts, out_ref = refs
            height = total * rows
            same = None
            for at in at_plane:
                side = jnp.concatenate([part[:, at].reshape(count * rows, columns) for part in parts], axis=0)
                product = lax.dot_general(
                    side, side, (((1,), (1,)), ((), ())), precision=HIGHEST, preferred_element_type=F32
                )
                same = product if same is None else same + product
            r = lax.broadcasted_iota(jnp.int32, (height, height), 0)
            c = lax.broadcasted_iota(jnp.int32, (height, height), 1)
            same = jnp.where(r % rows == c % rows, same, 0.0)
            pick = jnp.where(
                lax.broadcasted_iota(jnp.int32, (total, height), 1) // rows
                == lax.broadcasted_iota(jnp.int32, (total, height), 0),
                1.0,
                0.0,
            )
            half = jnp.dot(pick, same, precision=HIGHEST, preferred_element_type=F32)
            out_ref[...] = lax.dot_general(
                half, pick, (((1,), (1,)), ((), ())), precision=HIGHEST, preferred_element_type=F32
            )

        (gram_one,) = call(gram, [(total, total)], models, *others)
        if not halving:
            gram_one = lax.psum(gram_one, "slab")
        gram_pair = from_slab(gram_one, 1)

        def second_base(first, second, moved_ref, near_ref, far_ref, two_ref, base_out, inner_out):
            weights = plane_weights(rows, columns)
            masks = side_masks(rows, columns)

            def waves(p):
                for at, plane in zip(at_plane, inner_laplace(planes_of(two_ref[p], rows), weights)):
                    inner_out[p, at] = plane

            def adjoints(p):
                below, above = sides(masks, first, second, rows, p)
                later = 2.0 * near_ref[p].astype(F32) - far_ref[p].astype(F32)
                for z, plane in enumerate(inner_laplace(planes_of(moved_ref[p], rows), weights)):
                    at = at_plane[z]
                    base_out[p, at] = later[at] + plane + outer_laplace(below, above, z, layers)

            loop(count, waves)
            loop(count, adjoints)

        base, two_inner = call(
            second_base, [stack] * 2, near_first, near_second, near_moved, near, far, wave_two
        )

        def second(
            spots_ref,
            first,
            second,
            inner_ref,
            one_ref,
            two_ref,
            squared_ref,
            base_ref,
            gram_ref,
            pair_ref,
            lap_out,
            three_out,
            moved_out,
            gram_out,
        ):
            gram_out[...] = gram_ref[...] + pair_ref[...]
            masks = side_masks(rows, columns)

            def particle(p):
                below, above = sides(masks, first, second, rows, p)
                for z, at in enumerate(at_plane):
                    lap = inner_ref[p, at] + outer_laplace(below, above, z, layers)
                    lap_out[p, at] = lap
                    moved = squared_ref[p, at] * lap + spot(spots_ref, 4, z)
                    wave_three = 2.0 * two_ref[p, at] - one_ref[p, at] + moved
                    three = base_ref[p, at] - (spot(spots_ref, 0, z) * wave_three - spot(spots_ref, 2, z))
                    three_out[p, at] = three
                    moved_out[p, at] = squared_ref[p, at] * three

            loop(count, particle)

        lap_two, three, three_moved, gram_two = call(
            second,
            [stack] * 3 + [(total, total)],
            spots,
            two_first,
            two_second,
            two_inner,
            wave_one,
            wave_two,
            squared,
            base,
            gram_one,
            gram_pair,
        )
        gram_pair = from_slab(gram_two, 2)
        three_first, three_second = exchange(three_moved)

        def third_base(spots_ref, moved_ref, three_ref, near_ref, two_ref, lap_one_ref, lap_two_ref, out_ref):
            weights = plane_weights(rows, columns)

            def particle(p):
                before = near_ref[p].astype(F32)
                for z, lap in enumerate(inner_laplace(planes_of(moved_ref[p], rows), weights)):
                    at = at_plane[z]
                    three = three_ref[p, at]
                    injected = spot(spots_ref, 0, z) * two_ref[p, at] - spot(spots_ref, 1, z)
                    two = 2.0 * three - before[at] + lap - injected
                    out_ref[p, at] = two * lap_one_ref[p, at] + three * lap_two_ref[p, at]

            loop(count, particle)

        (inner_correlation,) = call(
            third_base,
            [stack],
            spots,
            three_moved,
            three,
            near,
            wave_two,
            lap_one,
            lap_two,
        )

        def third(first, second, inner_ref, lap_one_ref, squared_ref, gram_ref, pair_ref, out_ref, gram_out):
            gram_out[...] = gram_ref[...] + pair_ref[...]
            masks = side_masks(rows, columns)

            def particle(p):
                below, above = sides(masks, first, second, rows, p)
                for z, at in enumerate(at_plane):
                    full = inner_ref[p, at] + outer_laplace(below, above, z, layers) * lap_one_ref[p, at]
                    out_ref[p, at] = DATA_WEIGHT * squared_ref[p, at] * full

            loop(count, particle)

        pull, gram_full = call(
            third,
            [stack, (total, total)],
            three_first,
            three_second,
            inner_correlation,
            lap_one,
            squared,
            gram_two,
            gram_pair,
        )
        step = 4
        while halving and step < slabs:
            gram_full = gram_full + from_slab(gram_full, step)
            step *= 2
        far_pulls = [from_dom(pull, k) for k in range(1, doms)]
        pull_pair = other_shot(pull)

        def spread(gram_ref, out_ref):
            value = gram_ref[...]
            r = lax.broadcasted_iota(jnp.int32, (total, total), 0)
            c = lax.broadcasted_iota(jnp.int32, (total, total), 1)
            diagonal = jnp.where(r == c, value, 0.0)
            distance = jnp.sum(diagonal, axis=1, keepdims=True) + jnp.sum(diagonal, axis=0, keepdims=True) - 2.0 * value
            width = jnp.sum(jnp.sum(distance, axis=1, keepdims=True), axis=0, keepdims=True) / (
                total * (total - 1) * math.log(total)
            )
            kernel = jnp.exp(-distance / width)
            kernel = kernel / jnp.sum(kernel, axis=1, keepdims=True)
            for j in range(total):
                for i in range(count):
                    out_ref[j, i] = jnp.broadcast_to(kernel[i : i + 1, j : j + 1], (rows, columns))

        (spread_kernel,) = call(spread, [(total, count, rows, columns)], gram_full)

        def weigh(kernel_ref, start, pulled, z, values):
            for j in range(len(values)):
                for i in range(count):
                    pulled[i] = pulled[i] + kernel_ref[start + j, i] * values[j]
            return pulled

        def last_base(kernel_ref, pull_ref, pair_ref, *refs):
            *model_refs, out_ref = refs
            both = PRIOR_WEIGHT + REPEL_WEIGHT
            for at in at_plane:
                pulled = [REPEL_WEIGHT * model_refs[0][i, at] for i in range(count)]
                own = [pull_ref[j, at] + pair_ref[j, at] - both * model_refs[0][j, at] for j in range(count)]
                pulled = weigh(kernel_ref, 0, pulled, at, own)
                for k in range(1, doms):
                    pulled = weigh(kernel_ref, k * count, pulled, at, [-both * model_refs[k][j, at] for j in range(count)])
                for i in range(count):
                    out_ref[i, at] = pulled[i]

        (update_base,) = call(last_base, [stack], spread_kernel, pull, pull_pair, models, *others)

        def others_pull(kernel_ref, *refs):
            *pulls, out_ref = refs
            for at in at_plane:
                pulled = [jnp.zeros((rows, columns), F32)] * count
                for k, block in enumerate(pulls):
                    pulled = weigh(kernel_ref, (k + 1) * count, pulled, at, [block[j, at] for j in range(count)])
                for i in range(count):
                    out_ref[i, at] = pulled[i]

        (far_pull,) = call(others_pull, [stack], spread_kernel, *far_pulls)

        def last(base_ref, pull_ref, pair_ref, out_ref):
            out_ref[...] = base_ref[...] + (pull_ref[...] + pair_ref[...])

        (update,) = call(last, [stack], update_base, far_pull, other_shot(far_pull))
        return update.reshape(particles.shape)

    placed = (
        P(("grp", "dom"), "slab", None, None),
        P(("grp", "slab"), None, None),
        P(("grp", "dom"), "shot", "slab", None, None),
        P(("grp", "dom"), "shot", "slab", None, None),
        P(("grp", "dom"), "shot", "slab", None, None),
        P(("grp", "dom"), "shot", "slab", None, None),
        P(("grp", "shot")),
        P(("grp", "shot"), None),
        P(("grp", "shot"), None),
        P(("grp", "shot"), None, None),
    )
    return jax.shard_map(
        local,
        mesh=mesh,
        in_specs=placed,
        out_specs=P(("grp", "dom"), "slab", None, None),
        check_vma=False,
    )
```

```python
import functools
import math

import jax
import jax.numpy as jnp
from jax import lax
from jax.experimental import pallas as pl
from jax.experimental.pallas import tpu as pltpu
from jax.sharding import PartitionSpec as P

DATA_WEIGHT = 0.5
PRIOR_WEIGHT = 4.0
REPEL_WEIGHT = 4.0
STENCIL = (-205.0 / 72.0, 8.0 / 5.0, -1.0 / 5.0, 8.0 / 315.0, -1.0 / 560.0)
RADIUS = 4
F32 = jnp.float32
HIGHEST = lax.Precision.HIGHEST
LONG = 1 << 33


def call(body, outs, *operands, far=0, scratch=(), flops=1 << 20):
    moved = sum(x.size * x.dtype.itemsize for x in operands)
    outs = [x if isinstance(x, jax.ShapeDtypeStruct) else jax.ShapeDtypeStruct(x, F32) for x in outs]
    near = pl.BlockSpec(memory_space=pltpu.VMEM)
    operands = [pltpu.with_memory_space_constraint(x, pltpu.HBM) for x in operands[:far]] + list(operands[far:])
    return pl.pallas_call(
        body,
        out_shape=outs,
        in_specs=[pl.BlockSpec(memory_space=pltpu.HBM)] * far + [near] * (len(operands) - far),
        out_specs=[near] * len(outs),
        scratch_shapes=list(scratch),
        compiler_params=pltpu.CompilerParams(vmem_limit_bytes=24 << 20),
        cost_estimate=pl.CostEstimate(flops=flops, bytes_accessed=moved, transcendentals=0),
    )(*operands)


def fetch(sources, targets, semaphores):
    copies = [
        pltpu.make_async_copy(source, target, semaphores.at[k])
        for k, (source, target) in enumerate(zip(sources, targets))
    ]
    for copy in copies:
        copy.start()
    return copies


def plane_weights(rows, columns):
    x = lax.broadcasted_iota(jnp.int32, (rows, columns), 0)
    y = lax.broadcasted_iota(jnp.int32, (rows, columns), 1)
    found = []
    for axis, at, size in ((0, x, rows), (1, y, columns)):
        for shift in range(-RADIUS, RADIUS + 1):
            if shift:
                inside = (at + shift >= 0) & (at + shift < size)
                found.append((axis, (-shift) % size, jnp.where(inside, STENCIL[abs(shift)], 0.0)))
    return found


def inner_laplace(planes, weights):
    result = []
    for z, here in enumerate(planes):
        middle = (3.0 * STENCIL[0]) * here
        for other, plane in enumerate(planes):
            if other != z and abs(other - z) <= RADIUS:
                middle = middle + STENCIL[abs(other - z)] * plane
        parts = [middle]
        for low in range(0, len(weights), 4):
            some = None
            for axis, shift, weight in weights[low : low + 4]:
                term = weight * pltpu.roll(here, shift, axis)
                some = term if some is None else some + term
            parts.append(some)
        while len(parts) > 1:
            parts = [sum(parts[k : k + 2][1:], parts[k]) for k in range(0, len(parts), 2)]
        result.append(parts[0])
    return result


def outer_laplace(below, above, z, layers):
    total = None
    for j in range(RADIUS):
        for plane, distance in ((below[j], z + RADIUS - j), (above[j], layers + j - z)):
            if distance <= RADIUS:
                term = STENCIL[distance] * plane
                total = term if total is None else total + term
    return total


def planes_of(block, rows):
    return [block[z * rows : (z + 1) * rows] for z in range(block.shape[0] // rows)]


def side_masks(rows, columns):
    slab = jnp.full((rows, columns), lax.axis_index("slab"), jnp.int32)
    shot = jnp.full((rows, columns), lax.axis_index("shot"), jnp.int32)
    return shot > 0, slab > 0, slab < lax.axis_size("slab") - 1


def sides(masks, first, second, rows, p):
    turned, low_on, high_on = masks
    a, b = planes_of(first[p], rows), planes_of(second[p], rows)
    below = [jnp.where(low_on, jnp.where(turned, v, u), 0.0) for u, v in zip(a, b)]
    above = [jnp.where(high_on, jnp.where(turned, u, v), 0.0) for u, v in zip(a, b)]
    return below, above


def loop(count, body, together=2):
    if count % together:
        together = 1

    def step(group, carry):
        for p in range(together):
            body(group * together + p)
        return carry

    lax.fori_loop(0, count // together, step, 0)


def solution(mesh):
    slabs, doms = mesh.shape["slab"], mesh.shape["dom"]
    up = [(2 * z, 2 * z + 2) for z in range(slabs - 1)] + [(2 * slabs - 2, 2 * slabs - 1)]
    up += [(2 * z + 1, 2 * z - 1) for z in range(1, slabs)] + [(1, 0)]
    down = [(b, a) for a, b in up]

    def exchange(block):
        return lax.ppermute(block, ("slab", "shot"), up), lax.ppermute(block, ("slab", "shot"), down)

    def from_dom(block, distance):
        return lax.ppermute(block, "dom", [((i + distance) % doms, i) for i in range(doms)])

    def other_shot(block):
        return lax.ppermute(block, "shot", [(0, 1), (1, 0)])

    halving = slabs >= 4 and slabs & (slabs - 1) == 0

    def from_slab(block, step):
        if not halving:
            return jnp.zeros_like(block)
        return lax.ppermute(block, "slab", [(i, i ^ step) for i in range(slabs)])

    def local(
        particles,
        background,
        wave_prev,
        wave_now,
        adjoint_near,
        adjoint_far,
        sources,
        wavelet,
        receivers,
        observed,
    ):
        count, layers, rows, columns = particles.shape
        depth = layers * rows
        total = count * doms
        stack = (count, depth, columns)
        at_plane = [slice(z * rows, (z + 1) * rows) for z in range(layers)]
        models = particles.reshape(stack)
        ground = background.reshape(depth, columns)
        zero, one, near, far = (
            field.reshape(stack) for field in (wave_prev, wave_now, adjoint_near, adjoint_far)
        )

        halves = jax.ShapeDtypeStruct(stack, one.dtype)

        def prepare(one_hbm, models_hbm, ground_hbm, near_hbm, wave_ref, squared_ref, moved_ref, models_ref, near_ref, one_ref, ground_ref, arrived):
            copies = fetch(
                (one_hbm, models_hbm, ground_hbm, near_hbm), (one_ref, models_ref, ground_ref, near_ref), arrived
            )
            for copy in copies:
                copy.wait()

            def particle(p):
                wave_ref[p] = one_ref[p].astype(F32)
                squared = ground_ref[...] * jnp.exp(models_ref[p])
                squared_ref[p] = squared
                moved_ref[p] = squared * near_ref[p].astype(F32)

            loop(count, particle)

        wave_one, squared, near_moved, models, near = call(
            prepare,
            [stack] * 4 + [halves],
            one,
            models,
            ground,
            near,
            far=4,
            scratch=[
                pltpu.VMEM(stack, one.dtype),
                pltpu.VMEM((depth, columns), F32),
                pltpu.SemaphoreType.DMA((4,)),
            ],
        )
        one_first, one_second = exchange(wave_one)
        near_first, near_second = exchange(near_moved)

        def first_base(*refs):
            far_away, (source_ref, one_ref, inner_out, spots_out), held = refs[:5], refs[5:9], refs[9:14]
            wavelet_ref, receiver_ref, observed_ref = held[2:]
            copies = fetch(far_away, held, refs[14])
            weights = plane_weights(rows, columns)

            def particle(p):
                for at, plane in zip(at_plane, inner_laplace(planes_of(one_ref[p], rows), weights)):
                    inner_out[p, at] = plane

            loop(count, particle)
            for copy in copies:
                copy.wait()
            first_row = lax.axis_index("slab") * depth
            cells = receiver_ref[...]
            row = lax.shift_right_logical(cells, columns.bit_length() - 1) - first_row
            column = cells & (columns - 1)
            hit_row = lax.broadcasted_iota(jnp.int32, (depth, cells.shape[1]), 0) == row
            hit_column = lax.broadcasted_iota(jnp.int32, (columns, cells.shape[1]), 0) == column
            left = jnp.concatenate(
                [jnp.where(hit_row, value, 0.0) for value in (1.0, observed_ref[0:1], observed_ref[1:2])], axis=0
            )
            spots_out[0 : 3 * depth] = lax.dot_general(
                left,
                jnp.where(hit_column, 1.0, 0.0),
                (((1,), (1,)), ((), ())),
                precision=HIGHEST,
                preferred_element_type=F32,
            )
            cell = (lax.broadcasted_iota(jnp.int32, (depth, columns), 0) + first_row) * columns
            cell = cell + lax.broadcasted_iota(jnp.int32, (depth, columns), 1)
            at_source = cell == source_ref[0:1, :]
            spots_out[3 * depth : 4 * depth] = jnp.where(at_source, wavelet_ref[:, 0:1], 0.0)
            spots_out[4 * depth : 5 * depth] = jnp.where(at_source, wavelet_ref[:, 1:2], 0.0)

        small = (wavelet, receivers, observed.reshape(2, -1))
        one_inner, spots, zero, far = call(
            first_base,
            [stack, (5 * depth, columns), halves, halves],
            zero,
            far,
            *small,
            jnp.broadcast_to(sources[:, None], (rows, columns)),
            wave_one,
            far=5,
            scratch=[pltpu.VMEM(x.shape, x.dtype) for x in small] + [pltpu.SemaphoreType.DMA((5,))],
        )

        def spot(spots_ref, kind, z):
            return spots_ref[kind * depth + z * rows : kind * depth + (z + 1) * rows]

        def first(
            spots_ref, first, second, inner_ref, one_ref, zero_ref, squared_ref, models_ref, lap_out, wave_out, models_out
        ):
            models_out[...] = models_ref[...]
            masks = side_masks(rows, columns)

            def particle(p):
                below, above = sides(masks, first, second, rows, p)
                before = zero_ref[p].astype(F32)
                for z, at in enumerate(at_plane):
                    lap = inner_ref[p, at] + outer_laplace(below, above, z, layers)
                    lap_out[p, at] = lap
                    moved = squared_ref[p, at] * lap + spot(spots_ref, 3, z)
                    wave_out[p, at] = 2.0 * one_ref[p, at] - before[at] + moved

            loop(count, particle)

        lap_one, wave_two, models_sent = call(
            first, [stack] * 3, spots, one_first, one_second, one_inner, wave_one, zero, squared, models
        )
        two_first, two_second = exchange(wave_two)
        others = [from_dom(models_sent, k) for k in range(1, doms)]

        def second_base(first, second, moved_ref, near_ref, far_ref, two_ref, base_out, inner_out):
            weights = plane_weights(rows, columns)
            masks = side_masks(rows, columns)

            def waves(p):
                for at, plane in zip(at_plane, inner_laplace(planes_of(two_ref[p], rows), weights)):
                    inner_out[p, at] = plane

            def adjoints(p):
                below, above = sides(masks, first, second, rows, p)
                later = 2.0 * near_ref[p].astype(F32) - far_ref[p].astype(F32)
                for z, plane in enumerate(inner_laplace(planes_of(moved_ref[p], rows), weights)):
                    at = at_plane[z]
                    base_out[p, at] = later[at] + plane + outer_laplace(below, above, z, layers)

            loop(count, waves)
            loop(count, adjoints)

        base, two_inner = call(
            second_base, [stack] * 2, near_first, near_second, near_moved, near, far, wave_two
        )

        def second(
            spots_ref,
            first,
            second,
            inner_ref,
            one_ref,
            two_ref,
            squared_ref,
            base_ref,
            lap_out,
            three_out,
            moved_out,
        ):
            masks = side_masks(rows, columns)

            def particle(p):
                below, above = sides(masks, first, second, rows, p)
                for z, at in enumerate(at_plane):
                    lap = inner_ref[p, at] + outer_laplace(below, above, z, layers)
                    lap_out[p, at] = lap
                    moved = squared_ref[p, at] * lap + spot(spots_ref, 4, z)
                    wave_three = 2.0 * two_ref[p, at] - one_ref[p, at] + moved
                    three = base_ref[p, at] - (spot(spots_ref, 0, z) * wave_three - spot(spots_ref, 2, z))
                    three_out[p, at] = three
                    moved_out[p, at] = squared_ref[p, at] * three

            loop(count, particle)

        lap_two, three, three_moved = call(
            second,
            [stack] * 3,
            spots,
            two_first,
            two_second,
            two_inner,
            wave_one,
            wave_two,
            squared,
            base,
        )
        three_first, three_second = exchange(three_moved)

        wide = total * rows

        def gram(*refs):
            *parts, out_ref = refs
            side = jnp.concatenate(
                [
                    jnp.concatenate([part[:, at].reshape(count * rows, columns) for part in parts], axis=0)
                    for at in at_plane
                ],
                axis=1,
            )
            same = lax.dot_general(
                side, side, (((1,), (1,)), ((), ())), precision=HIGHEST, preferred_element_type=F32
            )
            r = lax.broadcasted_iota(jnp.int32, (wide, wide), 0)
            c = lax.broadcasted_iota(jnp.int32, (wide, wide), 1)
            same = jnp.where(r % rows == c % rows, same, 0.0)
            same = jnp.sum(same.reshape(total, rows, wide), axis=1)
            step = 1
            while step < rows:
                same = same + pltpu.roll(same, wide - step, 1)
                step *= 2
            first_of = lax.broadcasted_iota(jnp.int32, (total, wide), 1) % rows == 0
            out_ref[...] = jnp.where(first_of, same, 0.0)

        (gram_one,) = call(gram, [(total, wide)], models, *others)
        if not halving:
            gram_one = lax.psum(gram_one, "slab")
        gram_pair = from_slab(gram_one, 1)

        def third_base(spots_ref, moved_ref, three_ref, near_ref, two_ref, lap_one_ref, lap_two_ref, out_ref):
            weights = plane_weights(rows, columns)

            def particle(p):
                before = near_ref[p].astype(F32)
                for z, lap in enumerate(inner_laplace(planes_of(moved_ref[p], rows), weights)):
                    at = at_plane[z]
                    three = three_ref[p, at]
                    injected = spot(spots_ref, 0, z) * two_ref[p, at] - spot(spots_ref, 1, z)
                    two = 2.0 * three - before[at] + lap - injected
                    out_ref[p, at] = two * lap_one_ref[p, at] + three * lap_two_ref[p, at]

            loop(count, particle)

        (inner_correlation,) = call(
            third_base,
            [stack],
            spots,
            three_moved,
            three,
            near,
            wave_two,
            lap_one,
            lap_two,
        )

        def third(first, second, inner_ref, lap_one_ref, squared_ref, models_ref, out_ref):
            masks = side_masks(rows, columns)

            def particle(p):
                below, above = sides(masks, first, second, rows, p)
                for z, at in enumerate(at_plane):
                    full = inner_ref[p, at] + outer_laplace(below, above, z, layers) * lap_one_ref[p, at]
                    score = DATA_WEIGHT * squared_ref[p, at] * full
                    out_ref[p, at] = score - 0.5 * (PRIOR_WEIGHT + REPEL_WEIGHT) * models_ref[p, at]

            loop(count, particle)

        (pull,) = call(
            third,
            [stack],
            three_first,
            three_second,
            inner_correlation,
            lap_one,
            squared,
            models,
        )
        far_pulls = [from_dom(pull, k) for k in range(1, doms)]
        pull_pair = other_shot(pull)

        far_pairs = [other_shot(block) for block in far_pulls]

        def plus(first_ref, second_ref, out_ref):
            out_ref[...] = first_ref[...] + second_ref[...]

        step = 2
        while halving and step < slabs:
            (gram_one,) = call(plus, [(total, wide)], gram_one, gram_pair, flops=LONG)
            gram_pair = from_slab(gram_one, step)
            step *= 2

        def spread(gram_ref, pair_ref, out_ref):
            value = gram_ref[...] + pair_ref[...]
            r = lax.broadcasted_iota(jnp.int32, (total, wide), 0)
            c = lax.broadcasted_iota(jnp.int32, (total, wide), 1)
            diagonal = jnp.where(r * rows == c, value, 0.0)
            distance = jnp.sum(diagonal, axis=1, keepdims=True) + jnp.sum(diagonal, axis=0, keepdims=True) - 2.0 * value
            distance = jnp.where(c % rows == 0, distance, 0.0)
            width = jnp.sum(jnp.sum(distance, axis=1, keepdims=True), axis=0, keepdims=True) / (
                total * (total - 1) * math.log(total)
            )
            kernel = jnp.where(c % rows == 0, jnp.exp(-distance / width), 0.0)
            kernel = kernel / jnp.sum(kernel, axis=1, keepdims=True)
            for j in range(total):
                for i in range(count):
                    out_ref[j, i] = jnp.broadcast_to(kernel[i : i + 1, j * rows : j * rows + 1], (rows, columns))

        (spread_kernel,) = call(spread, [(total, count, rows, columns)], gram_one, gram_pair, flops=LONG)

        def weigh(kernel_ref, start, pulled, values):
            for j in range(len(values)):
                for i in range(count):
                    pulled[i] = pulled[i] + kernel_ref[start + j, i] * values[j]
            return pulled

        def last_base(kernel_ref, pull_ref, pair_ref, models_ref, out_ref):
            for at in at_plane:
                pulled = [REPEL_WEIGHT * models_ref[i, at] for i in range(count)]
                pulled = weigh(kernel_ref, 0, pulled, [pull_ref[j, at] + pair_ref[j, at] for j in range(count)])
                for i in range(count):
                    out_ref[i, at] = pulled[i]

        (update_base,) = call(last_base, [stack], spread_kernel, pull, pull_pair, models)

        def last(kernel_ref, base_ref, *refs):
            *pulls, out_ref = refs
            for at in at_plane:
                pulled = [base_ref[i, at] for i in range(count)]
                for k in range(1, doms):
                    here, there = pulls[k - 1], pulls[doms - 1 + k - 1]
                    pulled = weigh(kernel_ref, k * count, pulled, [here[j, at] + there[j, at] for j in range(count)])
                for i in range(count):
                    out_ref[i, at] = pulled[i]

        (update,) = call(last, [stack], spread_kernel, update_base, *far_pulls, *far_pairs)
        return update.reshape(particles.shape)

    placed = (
        P(("grp", "dom"), "slab", None, None),
        P(("grp", "slab"), None, None),
        P(("grp", "dom"), "shot", "slab", None, None),
        P(("grp", "dom"), "shot", "slab", None, None),
        P(("grp", "dom"), "shot", "slab", None, None),
        P(("grp", "dom"), "shot", "slab", None, None),
        P(("grp", "shot")),
        P(("grp", "shot"), None),
        P(("grp", "shot"), None),
        P(("grp", "shot"), None, None),
    )
    return jax.shard_map(
        local,
        mesh=mesh,
        in_specs=placed,
        out_specs=P(("grp", "dom"), "slab", None, None),
        check_vma=False,
    )
```

```python
import functools
import math

import jax
import jax.numpy as jnp
from jax import lax
from jax.experimental import pallas as pl
from jax.experimental.pallas import tpu as pltpu
from jax.sharding import PartitionSpec as P

DATA_WEIGHT = 0.5
PRIOR_WEIGHT = 4.0
REPEL_WEIGHT = 4.0
STENCIL = (-205.0 / 72.0, 8.0 / 5.0, -1.0 / 5.0, 8.0 / 315.0, -1.0 / 560.0)
RADIUS = 4
F32 = jnp.float32
HIGHEST = lax.Precision.HIGHEST
LONG = 1 << 33


def call(body, outs, *operands, far=0, scratch=(), flops=1 << 20):
    moved = sum(x.size * x.dtype.itemsize for x in operands)
    outs = [x if isinstance(x, jax.ShapeDtypeStruct) else jax.ShapeDtypeStruct(x, F32) for x in outs]
    near = pl.BlockSpec(memory_space=pltpu.VMEM)
    operands = [pltpu.with_memory_space_constraint(x, pltpu.HBM) for x in operands[:far]] + list(operands[far:])
    return pl.pallas_call(
        body,
        out_shape=outs,
        in_specs=[pl.BlockSpec(memory_space=pltpu.HBM)] * far + [near] * (len(operands) - far),
        out_specs=[near] * len(outs),
        scratch_shapes=list(scratch),
        compiler_params=pltpu.CompilerParams(vmem_limit_bytes=24 << 20),
        cost_estimate=pl.CostEstimate(flops=flops, bytes_accessed=moved, transcendentals=0),
    )(*operands)


def fetch(sources, targets, semaphores):
    copies = [
        pltpu.make_async_copy(source, target, semaphores.at[k])
        for k, (source, target) in enumerate(zip(sources, targets))
    ]
    for copy in copies:
        copy.start()
    return copies


def plane_weights(rows, columns):
    x = lax.broadcasted_iota(jnp.int32, (rows, columns), 0)
    y = lax.broadcasted_iota(jnp.int32, (rows, columns), 1)
    found = []
    for axis, at, size in ((0, x, rows), (1, y, columns)):
        for shift in range(-RADIUS, RADIUS + 1):
            if shift:
                inside = (at + shift >= 0) & (at + shift < size)
                found.append((axis, (-shift) % size, jnp.where(inside, STENCIL[abs(shift)], 0.0)))
    return found


def inner_laplace(planes, weights):
    result = []
    for z, here in enumerate(planes):
        middle = (3.0 * STENCIL[0]) * here
        for other, plane in enumerate(planes):
            if other != z and abs(other - z) <= RADIUS:
                middle = middle + STENCIL[abs(other - z)] * plane
        parts = [middle]
        for low in range(0, len(weights), 4):
            some = None
            for axis, shift, weight in weights[low : low + 4]:
                term = weight * pltpu.roll(here, shift, axis)
                some = term if some is None else some + term
            parts.append(some)
        while len(parts) > 1:
            parts = [sum(parts[k : k + 2][1:], parts[k]) for k in range(0, len(parts), 2)]
        result.append(parts[0])
    return result


def outer_laplace(below, above, z, layers):
    total = None
    for j in range(RADIUS):
        for plane, distance in ((below[j], z + RADIUS - j), (above[j], layers + j - z)):
            if distance <= RADIUS:
                term = STENCIL[distance] * plane
                total = term if total is None else total + term
    return total


def planes_of(block, rows):
    return [block[z * rows : (z + 1) * rows] for z in range(block.shape[0] // rows)]


def side_masks(rows, columns, flip=False):
    slab = jnp.full((rows, columns), lax.axis_index("slab"), jnp.int32)
    shot = jnp.full((rows, columns), lax.axis_index("shot"), jnp.int32)
    return (shot == 0 if flip else shot > 0), slab > 0, slab < lax.axis_size("slab") - 1


def sides(masks, first, second, rows, p):
    turned, low_on, high_on = masks
    a, b = planes_of(first[p], rows), planes_of(second[p], rows)
    below = [jnp.where(low_on, jnp.where(turned, v, u), 0.0) for u, v in zip(a, b)]
    above = [jnp.where(high_on, jnp.where(turned, u, v), 0.0) for u, v in zip(a, b)]
    return below, above


def loop(count, body, together=2):
    if count % together:
        together = 1

    def step(group, carry):
        for p in range(together):
            body(group * together + p)
        return carry

    lax.fori_loop(0, count // together, step, 0)


def solution(mesh):
    slabs, doms = mesh.shape["slab"], mesh.shape["dom"]
    up = [(2 * z, 2 * z + 2) for z in range(slabs - 1)] + [(2 * slabs - 2, 2 * slabs - 1)]
    up += [(2 * z + 1, 2 * z - 1) for z in range(1, slabs)] + [(1, 0)]
    down = [(b, a) for a, b in up]

    def exchange(block, flip=False):
        ways = (down, up) if flip else (up, down)
        return [lax.ppermute(block, ("slab", "shot"), way) for way in ways]

    def from_dom(block, distance):
        return lax.ppermute(block, "dom", [((i + distance) % doms, i) for i in range(doms)])

    def other_shot(block):
        return lax.ppermute(block, "shot", [(0, 1), (1, 0)])

    halving = slabs >= 4 and slabs & (slabs - 1) == 0

    def from_slab(block, step):
        if not halving:
            return jnp.zeros_like(block)
        return lax.ppermute(block, "slab", [(i, i ^ step) for i in range(slabs)])

    def local(
        particles,
        background,
        wave_prev,
        wave_now,
        adjoint_near,
        adjoint_far,
        sources,
        wavelet,
        receivers,
        observed,
    ):
        count, layers, rows, columns = particles.shape
        depth = layers * rows
        total = count * doms
        stack = (count, depth, columns)
        at_plane = [slice(z * rows, (z + 1) * rows) for z in range(layers)]
        models = particles.reshape(stack)
        ground = background.reshape(depth, columns)
        zero, one, near, far = (
            field.reshape(stack) for field in (wave_prev, wave_now, adjoint_near, adjoint_far)
        )

        halves = jax.ShapeDtypeStruct(stack, one.dtype)

        small = (wavelet, receivers, observed.reshape(2, -1))

        def prepare(*refs):
            sources_hbm, (wave_ref, squared_ref, moved_ref, models_ref, *kept), (one_ref, ground_ref, arrived) = (
                refs[:9],
                refs[9:19],
                refs[19:],
            )
            near_ref = kept[0]
            copies = fetch(sources_hbm, (one_ref, models_ref, ground_ref, *kept), arrived)
            for copy in copies[:4]:
                copy.wait()

            def particle(p):
                wave_ref[p] = one_ref[p].astype(F32)
                squared = ground_ref[...] * jnp.exp(models_ref[p])
                squared_ref[p] = squared
                moved_ref[p] = squared * near_ref[p].astype(F32)

            loop(count, particle)
            for copy in copies[4:]:
                copy.wait()

        wave_one, squared, near_moved, models, near, zero, far, *small = call(
            prepare,
            [stack] * 4 + [halves] * 3 + [jax.ShapeDtypeStruct(x.shape, x.dtype) for x in small],
            one,
            models,
            ground,
            near,
            zero,
            far,
            *small,
            far=9,
            scratch=[
                pltpu.VMEM(stack, one.dtype),
                pltpu.VMEM((depth, columns), F32),
                pltpu.SemaphoreType.DMA((9,)),
            ],
        )
        one_first, one_second = exchange(wave_one, flip=True)
        near_first, near_second = exchange(near_moved, flip=True)

        def first_base(source_ref, wavelet_ref, receiver_ref, observed_ref, one_ref, inner_out, spots_out):
            weights = plane_weights(rows, columns)

            def particle(p):
                for at, plane in zip(at_plane, inner_laplace(planes_of(one_ref[p], rows), weights)):
                    inner_out[p, at] = plane

            loop(count, particle)
            first_row = lax.axis_index("slab") * depth
            cells = receiver_ref[...]
            row = lax.shift_right_logical(cells, columns.bit_length() - 1) - first_row
            column = cells & (columns - 1)
            hit_row = lax.broadcasted_iota(jnp.int32, (depth, cells.shape[1]), 0) == row
            hit_column = lax.broadcasted_iota(jnp.int32, (columns, cells.shape[1]), 0) == column
            left = jnp.concatenate(
                [jnp.where(hit_row, value, 0.0) for value in (1.0, observed_ref[0:1], observed_ref[1:2])], axis=0
            )
            spots_out[0 : 3 * depth] = lax.dot_general(
                left,
                jnp.where(hit_column, 1.0, 0.0),
                (((1,), (1,)), ((), ())),
                precision=HIGHEST,
                preferred_element_type=F32,
            )
            cell = (lax.broadcasted_iota(jnp.int32, (depth, columns), 0) + first_row) * columns
            cell = cell + lax.broadcasted_iota(jnp.int32, (depth, columns), 1)
            at_source = cell == source_ref[0:1, :]
            spots_out[3 * depth : 4 * depth] = jnp.where(at_source, wavelet_ref[:, 0:1], 0.0)
            spots_out[4 * depth : 5 * depth] = jnp.where(at_source, wavelet_ref[:, 1:2], 0.0)

        one_inner, spots = call(
            first_base,
            [stack, (5 * depth, columns)],
            jnp.broadcast_to(sources[:, None], (rows, columns)),
            *small,
            wave_one,
        )

        def spot(spots_ref, kind, z):
            return spots_ref[kind * depth + z * rows : kind * depth + (z + 1) * rows]

        def first(
            spots_ref, first, second, inner_ref, one_ref, zero_ref, squared_ref, models_ref, lap_out, wave_out, models_out
        ):
            models_out[...] = models_ref[...]
            masks = side_masks(rows, columns, flip=True)

            def particle(p):
                below, above = sides(masks, first, second, rows, p)
                before = zero_ref[p].astype(F32)
                for z, at in enumerate(at_plane):
                    lap = inner_ref[p, at] + outer_laplace(below, above, z, layers)
                    lap_out[p, at] = lap
                    moved = squared_ref[p, at] * lap + spot(spots_ref, 3, z)
                    wave_out[p, at] = 2.0 * one_ref[p, at] - before[at] + moved

            loop(count, particle)

        lap_one, wave_two, models_sent = call(
            first, [stack] * 3, spots, one_first, one_second, one_inner, wave_one, zero, squared, models
        )
        two_first, two_second = exchange(wave_two)
        others = [from_dom(models_sent, k) for k in range(1, doms)]

        def second_base(first, second, moved_ref, near_ref, far_ref, two_ref, base_out, inner_out):
            weights = plane_weights(rows, columns)
            masks = side_masks(rows, columns, flip=True)

            def waves(p):
                for at, plane in zip(at_plane, inner_laplace(planes_of(two_ref[p], rows), weights)):
                    inner_out[p, at] = plane

            def adjoints(p):
                below, above = sides(masks, first, second, rows, p)
                later = 2.0 * near_ref[p].astype(F32) - far_ref[p].astype(F32)
                for z, plane in enumerate(inner_laplace(planes_of(moved_ref[p], rows), weights)):
                    at = at_plane[z]
                    base_out[p, at] = later[at] + plane + outer_laplace(below, above, z, layers)

            loop(count, waves)
            loop(count, adjoints)

        base, two_inner = call(
            second_base, [stack] * 2, near_first, near_second, near_moved, near, far, wave_two
        )

        def second(
            spots_ref,
            first,
            second,
            inner_ref,
            one_ref,
            two_ref,
            squared_ref,
            base_ref,
            lap_out,
            three_out,
            moved_out,
        ):
            masks = side_masks(rows, columns)

            def particle(p):
                below, above = sides(masks, first, second, rows, p)
                for z, at in enumerate(at_plane):
                    lap = inner_ref[p, at] + outer_laplace(below, above, z, layers)
                    lap_out[p, at] = lap
                    moved = squared_ref[p, at] * lap + spot(spots_ref, 4, z)
                    wave_three = 2.0 * two_ref[p, at] - one_ref[p, at] + moved
                    three = base_ref[p, at] - (spot(spots_ref, 0, z) * wave_three - spot(spots_ref, 2, z))
                    three_out[p, at] = three
                    moved_out[p, at] = squared_ref[p, at] * three

            loop(count, particle)

        lap_two, three, three_moved = call(
            second,
            [stack] * 3,
            spots,
            two_first,
            two_second,
            two_inner,
            wave_one,
            wave_two,
            squared,
            base,
        )
        three_first, three_second = exchange(three_moved)

        wide = total * rows

        def gram(*refs):
            *parts, out_ref = refs
            side = jnp.concatenate(
                [
                    jnp.concatenate([part[:, at].reshape(count * rows, columns) for part in parts], axis=0)
                    for at in at_plane
                ],
                axis=1,
            )
            same = lax.dot_general(
                side, side, (((1,), (1,)), ((), ())), precision=HIGHEST, preferred_element_type=F32
            )
            r = lax.broadcasted_iota(jnp.int32, (wide, wide), 0)
            c = lax.broadcasted_iota(jnp.int32, (wide, wide), 1)
            same = jnp.where(r % rows == c % rows, same, 0.0)
            same = jnp.sum(same.reshape(total, rows, wide), axis=1)
            step = 1
            while step < rows:
                same = same + pltpu.roll(same, wide - step, 1)
                step *= 2
            first_of = lax.broadcasted_iota(jnp.int32, (total, wide), 1) % rows == 0
            out_ref[...] = jnp.where(first_of, same, 0.0)

        (gram_one,) = call(gram, [(total, wide)], models, *others)
        if not halving:
            gram_one = lax.psum(gram_one, "slab")
        gram_pair = from_slab(gram_one, 1)

        def third_base(spots_ref, moved_ref, three_ref, near_ref, two_ref, lap_one_ref, lap_two_ref, out_ref):
            weights = plane_weights(rows, columns)

            def particle(p):
                before = near_ref[p].astype(F32)
                for z, lap in enumerate(inner_laplace(planes_of(moved_ref[p], rows), weights)):
                    at = at_plane[z]
                    three = three_ref[p, at]
                    injected = spot(spots_ref, 0, z) * two_ref[p, at] - spot(spots_ref, 1, z)
                    two = 2.0 * three - before[at] + lap - injected
                    out_ref[p, at] = two * lap_one_ref[p, at] + three * lap_two_ref[p, at]

            loop(count, particle)

        (inner_correlation,) = call(
            third_base,
            [stack],
            spots,
            three_moved,
            three,
            near,
            wave_two,
            lap_one,
            lap_two,
        )

        def third(first, second, inner_ref, lap_one_ref, squared_ref, models_ref, out_ref):
            masks = side_masks(rows, columns)

            def particle(p):
                below, above = sides(masks, first, second, rows, p)
                for z, at in enumerate(at_plane):
                    full = inner_ref[p, at] + outer_laplace(below, above, z, layers) * lap_one_ref[p, at]
                    score = DATA_WEIGHT * squared_ref[p, at] * full
                    out_ref[p, at] = score - 0.5 * (PRIOR_WEIGHT + REPEL_WEIGHT) * models_ref[p, at]

            loop(count, particle)

        (pull,) = call(
            third,
            [stack],
            three_first,
            three_second,
            inner_correlation,
            lap_one,
            squared,
            models,
        )
        far_pulls = [from_dom(pull, k) for k in range(1, doms)]
        pull_pair = other_shot(pull)

        far_pairs = [other_shot(block) for block in far_pulls]

        def plus(first_ref, second_ref, out_ref):
            out_ref[...] = first_ref[...] + second_ref[...]

        step = 2
        while halving and step < slabs:
            (gram_one,) = call(plus, [(total, wide)], gram_one, gram_pair, flops=LONG)
            gram_pair = from_slab(gram_one, step)
            step *= 2

        def spread(gram_ref, pair_ref, out_ref):
            value = gram_ref[...] + pair_ref[...]
            r = lax.broadcasted_iota(jnp.int32, (total, wide), 0)
            c = lax.broadcasted_iota(jnp.int32, (total, wide), 1)
            diagonal = jnp.where(r * rows == c, value, 0.0)
            distance = jnp.sum(diagonal, axis=1, keepdims=True) + jnp.sum(diagonal, axis=0, keepdims=True) - 2.0 * value
            distance = jnp.where(c % rows == 0, distance, 0.0)
            width = jnp.sum(jnp.sum(distance, axis=1, keepdims=True), axis=0, keepdims=True) / (
                total * (total - 1) * math.log(total)
            )
            kernel = jnp.where(c % rows == 0, jnp.exp(-distance / width), 0.0)
            kernel = kernel / jnp.sum(kernel, axis=1, keepdims=True)
            for j in range(total):
                for i in range(count):
                    out_ref[j, i] = jnp.broadcast_to(kernel[i : i + 1, j * rows : j * rows + 1], (rows, columns))

        (spread_kernel,) = call(spread, [(total, count, rows, columns)], gram_one, gram_pair, flops=LONG)

        def weigh(kernel_ref, start, pulled, values):
            for j in range(len(values)):
                for i in range(count):
                    pulled[i] = pulled[i] + kernel_ref[start + j, i] * values[j]
            return pulled

        def last_base(kernel_ref, pull_ref, pair_ref, models_ref, out_ref):
            for at in at_plane:
                pulled = [REPEL_WEIGHT * models_ref[i, at] for i in range(count)]
                pulled = weigh(kernel_ref, 0, pulled, [pull_ref[j, at] + pair_ref[j, at] for j in range(count)])
                for i in range(count):
                    out_ref[i, at] = pulled[i]

        (update_base,) = call(last_base, [stack], spread_kernel, pull, pull_pair, models)

        def last(kernel_ref, base_ref, *refs):
            *pulls, out_ref = refs
            for at in at_plane:
                pulled = [base_ref[i, at] for i in range(count)]
                for k in range(1, doms):
                    here, there = pulls[k - 1], pulls[doms - 1 + k - 1]
                    pulled = weigh(kernel_ref, k * count, pulled, [here[j, at] + there[j, at] for j in range(count)])
                for i in range(count):
                    out_ref[i, at] = pulled[i]

        (update,) = call(last, [stack], spread_kernel, update_base, *far_pulls, *far_pairs)
        return update.reshape(particles.shape)

    placed = (
        P(("grp", "dom"), "slab", None, None),
        P(("grp", "slab"), None, None),
        P(("grp", "dom"), "shot", "slab", None, None),
        P(("grp", "dom"), "shot", "slab", None, None),
        P(("grp", "dom"), "shot", "slab", None, None),
        P(("grp", "dom"), "shot", "slab", None, None),
        P(("grp", "shot")),
        P(("grp", "shot"), None),
        P(("grp", "shot"), None),
        P(("grp", "shot"), None, None),
    )
    return jax.shard_map(
        local,
        mesh=mesh,
        in_specs=placed,
        out_specs=P(("grp", "dom"), "slab", None, None),
        check_vma=False,
    )
```

```python
import functools
import math

import jax
import jax.numpy as jnp
from jax import lax
from jax.experimental import pallas as pl
from jax.experimental.pallas import tpu as pltpu
from jax.sharding import PartitionSpec as P

DATA_WEIGHT = 0.5
PRIOR_WEIGHT = 4.0
REPEL_WEIGHT = 4.0
STENCIL = (-205.0 / 72.0, 8.0 / 5.0, -1.0 / 5.0, 8.0 / 315.0, -1.0 / 560.0)
RADIUS = 4
F32 = jnp.float32
HIGHEST = lax.Precision.HIGHEST
LONG = 1 << 33


def call(body, outs, *operands, far=0, scratch=(), flops=1 << 20):
    moved = sum(x.size * x.dtype.itemsize for x in operands)
    outs = [x if isinstance(x, jax.ShapeDtypeStruct) else jax.ShapeDtypeStruct(x, F32) for x in outs]
    near = pl.BlockSpec(memory_space=pltpu.VMEM)
    operands = [pltpu.with_memory_space_constraint(x, pltpu.HBM) for x in operands[:far]] + list(operands[far:])
    return pl.pallas_call(
        body,
        out_shape=outs,
        in_specs=[pl.BlockSpec(memory_space=pltpu.HBM)] * far + [near] * (len(operands) - far),
        out_specs=[near] * len(outs),
        scratch_shapes=list(scratch),
        compiler_params=pltpu.CompilerParams(vmem_limit_bytes=24 << 20),
        cost_estimate=pl.CostEstimate(flops=flops, bytes_accessed=moved, transcendentals=0),
    )(*operands)


def fetch(sources, targets, semaphores):
    copies = [
        pltpu.make_async_copy(source, target, semaphores.at[k])
        for k, (source, target) in enumerate(zip(sources, targets))
    ]
    for copy in copies:
        copy.start()
    return copies


def plane_weights(rows, columns):
    x = lax.broadcasted_iota(jnp.int32, (rows, columns), 0)
    y = lax.broadcasted_iota(jnp.int32, (rows, columns), 1)
    found = []
    for axis, at, size in ((0, x, rows), (1, y, columns)):
        for shift in range(-RADIUS, RADIUS + 1):
            if shift:
                inside = (at + shift >= 0) & (at + shift < size)
                found.append((axis, (-shift) % size, jnp.where(inside, STENCIL[abs(shift)], 0.0)))
    return found


def inner_laplace(planes, weights):
    result = []
    for z, here in enumerate(planes):
        middle = (3.0 * STENCIL[0]) * here
        for other, plane in enumerate(planes):
            if other != z and abs(other - z) <= RADIUS:
                middle = middle + STENCIL[abs(other - z)] * plane
        parts = [middle]
        for low in range(0, len(weights), 4):
            some = None
            for axis, shift, weight in weights[low : low + 4]:
                term = weight * pltpu.roll(here, shift, axis)
                some = term if some is None else some + term
            parts.append(some)
        while len(parts) > 1:
            parts = [sum(parts[k : k + 2][1:], parts[k]) for k in range(0, len(parts), 2)]
        result.append(parts[0])
    return result


def outer_laplace(below, above, z, layers):
    total = None
    for j in range(RADIUS):
        for plane, distance in ((below[j], z + RADIUS - j), (above[j], layers + j - z)):
            if distance <= RADIUS:
                term = STENCIL[distance] * plane
                total = term if total is None else total + term
    return total


def planes_of(block, rows):
    return [block[z * rows : (z + 1) * rows] for z in range(block.shape[0] // rows)]


def side_masks(rows, columns, flip=False):
    slab = jnp.full((rows, columns), lax.axis_index("slab"), jnp.int32)
    shot = jnp.full((rows, columns), lax.axis_index("shot"), jnp.int32)
    return (shot == 0 if flip else shot > 0), slab > 0, slab < lax.axis_size("slab") - 1


def sides(masks, first, second, rows, p):
    turned, low_on, high_on = masks
    a, b = planes_of(first[p], rows), planes_of(second[p], rows)
    below = [jnp.where(low_on, jnp.where(turned, v, u), 0.0) for u, v in zip(a, b)]
    above = [jnp.where(high_on, jnp.where(turned, u, v), 0.0) for u, v in zip(a, b)]
    return below, above


def loop(count, body, together=2):
    if count % together:
        together = 1

    def step(group, carry):
        for p in range(together):
            body(group * together + p)
        return carry

    lax.fori_loop(0, count // together, step, 0)


def solution(mesh):
    slabs, doms = mesh.shape["slab"], mesh.shape["dom"]
    up = [(2 * z, 2 * z + 2) for z in range(slabs - 1)] + [(2 * slabs - 2, 2 * slabs - 1)]
    up += [(2 * z + 1, 2 * z - 1) for z in range(1, slabs)] + [(1, 0)]
    down = [(b, a) for a, b in up]

    def exchange(block, flip=False):
        ways = (down, up) if flip else (up, down)
        return [lax.ppermute(block, ("slab", "shot"), way) for way in ways]

    def from_dom(block, distance):
        return lax.ppermute(block, "dom", [((i + distance) % doms, i) for i in range(doms)])

    def other_shot(block):
        return lax.ppermute(block, "shot", [(0, 1), (1, 0)])

    halving = slabs >= 4 and slabs & (slabs - 1) == 0

    def from_slab(block, step):
        if not halving:
            return jnp.zeros_like(block)
        return lax.ppermute(block, "slab", [(i, i ^ step) for i in range(slabs)])

    def local(
        particles,
        background,
        wave_prev,
        wave_now,
        adjoint_near,
        adjoint_far,
        sources,
        wavelet,
        receivers,
        observed,
    ):
        count, layers, rows, columns = particles.shape
        depth = layers * rows
        total = count * doms
        stack = (count, depth, columns)
        at_plane = [slice(z * rows, (z + 1) * rows) for z in range(layers)]
        models = particles.reshape(stack)
        ground = background.reshape(depth, columns)
        zero, one, near, far = (
            field.reshape(stack) for field in (wave_prev, wave_now, adjoint_near, adjoint_far)
        )

        halves = jax.ShapeDtypeStruct(stack, one.dtype)

        small = (wavelet, receivers, observed.reshape(2, -1))

        def prepare(*refs):
            sources_hbm, (wave_ref, squared_ref, moved_ref, models_ref, *kept), (one_ref, ground_ref, arrived) = (
                refs[:9],
                refs[9:19],
                refs[19:],
            )
            near_ref = kept[0]
            copies = fetch(sources_hbm, (one_ref, models_ref, ground_ref, *kept), arrived)
            for copy in copies[:4]:
                copy.wait()

            def particle(p):
                wave_ref[p] = one_ref[p].astype(F32)
                squared = ground_ref[...] * jnp.exp(models_ref[p])
                squared_ref[p] = squared
                moved_ref[p] = squared * near_ref[p].astype(F32)

            loop(count, particle)
            for copy in copies[4:]:
                copy.wait()

        wave_one, squared, near_moved, models, near, zero, far, *small = call(
            prepare,
            [stack] * 4 + [halves] * 3 + [jax.ShapeDtypeStruct(x.shape, x.dtype) for x in small],
            one,
            models,
            ground,
            near,
            zero,
            far,
            *small,
            far=9,
            scratch=[
                pltpu.VMEM(stack, one.dtype),
                pltpu.VMEM((depth, columns), F32),
                pltpu.SemaphoreType.DMA((9,)),
            ],
        )
        one_first, one_second = exchange(wave_one, flip=True)
        near_first, near_second = exchange(near_moved, flip=True)

        def first_base(source_ref, wavelet_ref, receiver_ref, observed_ref, one_ref, inner_out, spots_out):
            weights = plane_weights(rows, columns)

            def particle(p):
                for at, plane in zip(at_plane, inner_laplace(planes_of(one_ref[p], rows), weights)):
                    inner_out[p, at] = plane

            loop(count, particle)
            first_row = lax.axis_index("slab") * depth
            cells = receiver_ref[...]
            row = lax.shift_right_logical(cells, columns.bit_length() - 1) - first_row
            column = cells & (columns - 1)
            hit_row = lax.broadcasted_iota(jnp.int32, (depth, cells.shape[1]), 0) == row
            hit_column = lax.broadcasted_iota(jnp.int32, (columns, cells.shape[1]), 0) == column
            left = jnp.concatenate(
                [jnp.where(hit_row, value, 0.0) for value in (1.0, observed_ref[0:1], observed_ref[1:2])], axis=0
            )
            spots_out[0 : 3 * depth] = lax.dot_general(
                left,
                jnp.where(hit_column, 1.0, 0.0),
                (((1,), (1,)), ((), ())),
                precision=HIGHEST,
                preferred_element_type=F32,
            )
            cell = (lax.broadcasted_iota(jnp.int32, (depth, columns), 0) + first_row) * columns
            cell = cell + lax.broadcasted_iota(jnp.int32, (depth, columns), 1)
            at_source = cell == source_ref[0:1, :]
            spots_out[3 * depth : 4 * depth] = jnp.where(at_source, wavelet_ref[:, 0:1], 0.0)
            spots_out[4 * depth : 5 * depth] = jnp.where(at_source, wavelet_ref[:, 1:2], 0.0)

        one_inner, spots = call(
            first_base,
            [stack, (5 * depth, columns)],
            jnp.broadcast_to(sources[:, None], (rows, columns)),
            *small,
            wave_one,
        )

        def spot(spots_ref, kind, z):
            return spots_ref[kind * depth + z * rows : kind * depth + (z + 1) * rows]

        def first(
            spots_ref, first, second, inner_ref, one_ref, zero_ref, squared_ref, models_ref, lap_out, wave_out, models_out
        ):
            models_out[...] = models_ref[...]
            masks = side_masks(rows, columns, flip=True)

            def particle(p):
                below, above = sides(masks, first, second, rows, p)
                before = zero_ref[p].astype(F32)
                for z, at in enumerate(at_plane):
                    lap = inner_ref[p, at] + outer_laplace(below, above, z, layers)
                    lap_out[p, at] = lap
                    moved = squared_ref[p, at] * lap + spot(spots_ref, 3, z)
                    wave_out[p, at] = 2.0 * one_ref[p, at] - before[at] + moved

            loop(count, particle)

        lap_one, wave_two, models_sent = call(
            first, [stack] * 3, spots, one_first, one_second, one_inner, wave_one, zero, squared, models
        )
        two_first, two_second = exchange(wave_two)
        others = [from_dom(models_sent, k) for k in range(1, doms)]

        def second_base(first, second, moved_ref, near_ref, far_ref, two_ref, base_out, inner_out):
            weights = plane_weights(rows, columns)
            masks = side_masks(rows, columns, flip=True)

            def waves(p):
                for at, plane in zip(at_plane, inner_laplace(planes_of(two_ref[p], rows), weights)):
                    inner_out[p, at] = plane

            def adjoints(p):
                below, above = sides(masks, first, second, rows, p)
                later = 2.0 * near_ref[p].astype(F32) - far_ref[p].astype(F32)
                for z, plane in enumerate(inner_laplace(planes_of(moved_ref[p], rows), weights)):
                    at = at_plane[z]
                    base_out[p, at] = later[at] + plane + outer_laplace(below, above, z, layers)

            loop(count, waves)
            loop(count, adjoints)

        base, two_inner = call(
            second_base, [stack] * 2, near_first, near_second, near_moved, near, far, wave_two
        )

        def second(
            spots_ref,
            first,
            second,
            inner_ref,
            one_ref,
            two_ref,
            squared_ref,
            base_ref,
            lap_out,
            three_out,
            moved_out,
        ):
            masks = side_masks(rows, columns)

            def particle(p):
                below, above = sides(masks, first, second, rows, p)
                for z, at in enumerate(at_plane):
                    lap = inner_ref[p, at] + outer_laplace(below, above, z, layers)
                    lap_out[p, at] = lap
                    moved = squared_ref[p, at] * lap + spot(spots_ref, 4, z)
                    wave_three = 2.0 * two_ref[p, at] - one_ref[p, at] + moved
                    three = base_ref[p, at] - (spot(spots_ref, 0, z) * wave_three - spot(spots_ref, 2, z))
                    three_out[p, at] = three
                    moved_out[p, at] = squared_ref[p, at] * three

            loop(count, particle)

        lap_two, three, three_moved = call(
            second,
            [stack] * 3,
            spots,
            two_first,
            two_second,
            two_inner,
            wave_one,
            wave_two,
            squared,
            base,
        )
        three_first, three_second = exchange(three_moved)

        wide = total * rows

        def gram(*refs):
            *parts, out_ref = refs
            side = jnp.concatenate(
                [
                    jnp.concatenate([part[:, at].reshape(count * rows, columns) for part in parts], axis=0)
                    for at in at_plane
                ],
                axis=1,
            )
            same = lax.dot_general(
                side, side, (((1,), (1,)), ((), ())), precision=HIGHEST, preferred_element_type=F32
            )
            r = lax.broadcasted_iota(jnp.int32, (wide, wide), 0)
            c = lax.broadcasted_iota(jnp.int32, (wide, wide), 1)
            same = jnp.where(r % rows == c % rows, same, 0.0)
            same = jnp.sum(same.reshape(total, rows, wide), axis=1)
            step = 1
            while step < rows:
                same = same + pltpu.roll(same, wide - step, 1)
                step *= 2
            first_of = lax.broadcasted_iota(jnp.int32, (total, wide), 1) % rows == 0
            out_ref[...] = jnp.where(first_of, same, 0.0)

        (gram_one,) = call(gram, [(total, wide)], models, *others)
        if not halving:
            gram_one = lax.psum(gram_one, "slab")
        gram_pair = from_slab(gram_one, 2)

        def third_base(spots_ref, moved_ref, three_ref, near_ref, two_ref, lap_one_ref, lap_two_ref, out_ref):
            weights = plane_weights(rows, columns)

            def particle(p):
                before = near_ref[p].astype(F32)
                for z, lap in enumerate(inner_laplace(planes_of(moved_ref[p], rows), weights)):
                    at = at_plane[z]
                    three = three_ref[p, at]
                    injected = spot(spots_ref, 0, z) * two_ref[p, at] - spot(spots_ref, 1, z)
                    two = 2.0 * three - before[at] + lap - injected
                    out_ref[p, at] = two * lap_one_ref[p, at] + three * lap_two_ref[p, at]

            loop(count, particle)

        (inner_correlation,) = call(
            third_base,
            [stack],
            spots,
            three_moved,
            three,
            near,
            wave_two,
            lap_one,
            lap_two,
        )

        def third(first, second, inner_ref, lap_one_ref, squared_ref, models_ref, out_ref):
            masks = side_masks(rows, columns)

            def particle(p):
                below, above = sides(masks, first, second, rows, p)
                for z, at in enumerate(at_plane):
                    full = inner_ref[p, at] + outer_laplace(below, above, z, layers) * lap_one_ref[p, at]
                    score = DATA_WEIGHT * squared_ref[p, at] * full
                    out_ref[p, at] = score - 0.5 * (PRIOR_WEIGHT + REPEL_WEIGHT) * models_ref[p, at]

            loop(count, particle)

        (pull,) = call(
            third,
            [stack],
            three_first,
            three_second,
            inner_correlation,
            lap_one,
            squared,
            models,
        )
        far_pulls = [from_dom(pull, k) for k in range(1, doms)]
        pull_pair = other_shot(pull)

        far_pairs = [other_shot(block) for block in far_pulls]

        def plus(first_ref, second_ref, out_ref):
            out_ref[...] = first_ref[...] + second_ref[...]

        step = 2
        while halving and step < slabs:
            (gram_one,) = call(plus, [(total, wide)], gram_one, gram_pair, flops=LONG)
            gram_pair = from_slab(gram_one, 1 if step == 2 else step)
            step *= 2

        def spread(gram_ref, pair_ref, out_ref):
            value = gram_ref[...] + pair_ref[...]
            r = lax.broadcasted_iota(jnp.int32, (total, wide), 0)
            c = lax.broadcasted_iota(jnp.int32, (total, wide), 1)
            diagonal = jnp.where(r * rows == c, value, 0.0)
            distance = jnp.sum(diagonal, axis=1, keepdims=True) + jnp.sum(diagonal, axis=0, keepdims=True) - 2.0 * value
            distance = jnp.where(c % rows == 0, distance, 0.0)
            width = jnp.sum(jnp.sum(distance, axis=1, keepdims=True), axis=0, keepdims=True) / (
                total * (total - 1) * math.log(total)
            )
            kernel = jnp.where(c % rows == 0, jnp.exp(-distance / width), 0.0)
            kernel = kernel / jnp.sum(kernel, axis=1, keepdims=True)
            for j in range(total):
                out_ref[j] = jnp.broadcast_to(kernel[:count, j * rows : j * rows + 1], (count, columns))

        (spread_kernel,) = call(spread, [(total, count, columns)], gram_one, gram_pair, flops=LONG)

        def weigh(kernel_ref, start, pulled, values):
            for j in range(len(values)):
                for i in range(count):
                    pulled[i] = pulled[i] + kernel_ref[start + j, i : i + 1] * values[j]
            return pulled

        def last_base(kernel_ref, pull_ref, pair_ref, models_ref, out_ref):
            for at in at_plane:
                pulled = [REPEL_WEIGHT * models_ref[i, at] for i in range(count)]
                pulled = weigh(kernel_ref, 0, pulled, [pull_ref[j, at] + pair_ref[j, at] for j in range(count)])
                for i in range(count):
                    out_ref[i, at] = pulled[i]

        (update_base,) = call(last_base, [stack], spread_kernel, pull, pull_pair, models)

        def last(kernel_ref, base_ref, *refs):
            *pulls, out_ref = refs
            for at in at_plane:
                pulled = [base_ref[i, at] for i in range(count)]
                for k in range(1, doms):
                    here, there = pulls[k - 1], pulls[doms - 1 + k - 1]
                    pulled = weigh(kernel_ref, k * count, pulled, [here[j, at] + there[j, at] for j in range(count)])
                for i in range(count):
                    out_ref[i, at] = pulled[i]

        (update,) = call(last, [stack], spread_kernel, update_base, *far_pulls, *far_pairs)
        return update.reshape(particles.shape)

    placed = (
        P(("grp", "dom"), "slab", None, None),
        P(("grp", "slab"), None, None),
        P(("grp", "dom"), "shot", "slab", None, None),
        P(("grp", "dom"), "shot", "slab", None, None),
        P(("grp", "dom"), "shot", "slab", None, None),
        P(("grp", "dom"), "shot", "slab", None, None),
        P(("grp", "shot")),
        P(("grp", "shot"), None),
        P(("grp", "shot"), None),
        P(("grp", "shot"), None, None),
    )
    return jax.shard_map(
        local,
        mesh=mesh,
        in_specs=placed,
        out_specs=P(("grp", "dom"), "slab", None, None),
        check_vma=False,
    )
```

```python
import functools
import math

import jax
import jax.numpy as jnp
from jax import lax
from jax.experimental import pallas as pl
from jax.experimental.pallas import tpu as pltpu
from jax.sharding import PartitionSpec as P

DATA_WEIGHT = 0.5
PRIOR_WEIGHT = 4.0
REPEL_WEIGHT = 4.0
STENCIL = (-205.0 / 72.0, 8.0 / 5.0, -1.0 / 5.0, 8.0 / 315.0, -1.0 / 560.0)
RADIUS = 4
F32 = jnp.float32
HIGHEST = lax.Precision.HIGHEST
LONG = 1 << 33


def call(body, outs, *operands, far=0, scratch=(), flops=1 << 20):
    moved = sum(x.size * x.dtype.itemsize for x in operands)
    outs = [x if isinstance(x, jax.ShapeDtypeStruct) else jax.ShapeDtypeStruct(x, F32) for x in outs]
    near = pl.BlockSpec(memory_space=pltpu.VMEM)
    operands = [pltpu.with_memory_space_constraint(x, pltpu.HBM) for x in operands[:far]] + list(operands[far:])
    return pl.pallas_call(
        body,
        out_shape=outs,
        in_specs=[pl.BlockSpec(memory_space=pltpu.HBM)] * far + [near] * (len(operands) - far),
        out_specs=[near] * len(outs),
        scratch_shapes=list(scratch),
        compiler_params=pltpu.CompilerParams(vmem_limit_bytes=24 << 20),
        cost_estimate=pl.CostEstimate(flops=flops, bytes_accessed=moved, transcendentals=0),
    )(*operands)


def fetch(sources, targets, semaphores):
    copies = [
        pltpu.make_async_copy(source, target, semaphores.at[k])
        for k, (source, target) in enumerate(zip(sources, targets))
    ]
    for copy in copies:
        copy.start()
    return copies


def plane_weights(rows, columns):
    x = lax.broadcasted_iota(jnp.int32, (rows, columns), 0)
    y = lax.broadcasted_iota(jnp.int32, (rows, columns), 1)
    found = []
    for axis, at, size in ((0, x, rows), (1, y, columns)):
        for shift in range(-RADIUS, RADIUS + 1):
            if shift:
                inside = (at + shift >= 0) & (at + shift < size)
                found.append((axis, (-shift) % size, jnp.where(inside, STENCIL[abs(shift)], 0.0)))
    return found


def inner_laplace(planes, weights):
    result = []
    for z, here in enumerate(planes):
        middle = (3.0 * STENCIL[0]) * here
        for other, plane in enumerate(planes):
            if other != z and abs(other - z) <= RADIUS:
                middle = middle + STENCIL[abs(other - z)] * plane
        parts = [middle]
        for low in range(0, len(weights), 4):
            some = None
            for axis, shift, weight in weights[low : low + 4]:
                term = weight * pltpu.roll(here, shift, axis)
                some = term if some is None else some + term
            parts.append(some)
        while len(parts) > 1:
            parts = [sum(parts[k : k + 2][1:], parts[k]) for k in range(0, len(parts), 2)]
        result.append(parts[0])
    return result


def outer_laplace(below, above, z, layers):
    total = None
    for j in range(RADIUS):
        for plane, distance in ((below[j], z + RADIUS - j), (above[j], layers + j - z)):
            if distance <= RADIUS:
                term = STENCIL[distance] * plane
                total = term if total is None else total + term
    return total


def planes_of(block, rows):
    return [block[z * rows : (z + 1) * rows] for z in range(block.shape[0] // rows)]


def side_masks(rows, columns, flip=False):
    slab = jnp.full((rows, columns), lax.axis_index("slab"), jnp.int32)
    shot = jnp.full((rows, columns), lax.axis_index("shot"), jnp.int32)
    return (shot == 0 if flip else shot > 0), slab > 0, slab < lax.axis_size("slab") - 1


def sides(masks, first, second, rows, p):
    turned, low_on, high_on = masks
    a, b = planes_of(first[p], rows), planes_of(second[p], rows)
    below = [jnp.where(low_on, jnp.where(turned, v, u), 0.0) for u, v in zip(a, b)]
    above = [jnp.where(high_on, jnp.where(turned, u, v), 0.0) for u, v in zip(a, b)]
    return below, above


def loop(count, body, together=8):
    if count % together:
        together = 1

    def step(group, carry):
        for p in range(together):
            body(group * together + p)
        return carry

    lax.fori_loop(0, count // together, step, 0)


def solution(mesh):
    slabs, doms = mesh.shape["slab"], mesh.shape["dom"]
    up = [(2 * z, 2 * z + 2) for z in range(slabs - 1)] + [(2 * slabs - 2, 2 * slabs - 1)]
    up += [(2 * z + 1, 2 * z - 1) for z in range(1, slabs)] + [(1, 0)]
    down = [(b, a) for a, b in up]

    def exchange(block, flip=False):
        ways = (down, up) if flip else (up, down)
        return [lax.ppermute(block, ("slab", "shot"), way) for way in ways]

    def from_dom(block, distance):
        return lax.ppermute(block, "dom", [((i + distance) % doms, i) for i in range(doms)])

    def other_shot(block):
        return lax.ppermute(block, "shot", [(0, 1), (1, 0)])

    halving = slabs >= 4 and slabs & (slabs - 1) == 0

    def from_slab(block, step):
        if not halving:
            return jnp.zeros_like(block)
        return lax.ppermute(block, "slab", [(i, i ^ step) for i in range(slabs)])

    def local(
        particles,
        background,
        wave_prev,
        wave_now,
        adjoint_near,
        adjoint_far,
        sources,
        wavelet,
        receivers,
        observed,
    ):
        count, layers, rows, columns = particles.shape
        depth = layers * rows
        total = count * doms
        stack = (count, depth, columns)
        at_plane = [slice(z * rows, (z + 1) * rows) for z in range(layers)]
        models = particles.reshape(stack)
        ground = background.reshape(depth, columns)
        zero, one, near, far = (
            field.reshape(stack) for field in (wave_prev, wave_now, adjoint_near, adjoint_far)
        )

        halves = jax.ShapeDtypeStruct(stack, one.dtype)

        small = (wavelet, receivers, observed.reshape(2, -1))

        def prepare(*refs):
            sources_hbm, (wave_ref, squared_ref, moved_ref, models_ref, *kept), (one_ref, ground_ref, arrived) = (
                refs[:9],
                refs[9:19],
                refs[19:],
            )
            near_ref = kept[0]
            copies = fetch(sources_hbm, (one_ref, models_ref, ground_ref, *kept), arrived)
            for copy in copies[:4]:
                copy.wait()

            def particle(p):
                wave_ref[p] = one_ref[p].astype(F32)
                squared = ground_ref[...] * jnp.exp(models_ref[p])
                squared_ref[p] = squared
                moved_ref[p] = squared * near_ref[p].astype(F32)

            loop(count, particle)
            for copy in copies[4:]:
                copy.wait()

        wave_one, squared, near_moved, models, near, zero, far, *small = call(
            prepare,
            [stack] * 4 + [halves] * 3 + [jax.ShapeDtypeStruct(x.shape, x.dtype) for x in small],
            one,
            models,
            ground,
            near,
            zero,
            far,
            *small,
            far=9,
            scratch=[
                pltpu.VMEM(stack, one.dtype),
                pltpu.VMEM((depth, columns), F32),
                pltpu.SemaphoreType.DMA((9,)),
            ],
        )
        one_first, one_second = exchange(wave_one, flip=True)
        near_first, near_second = exchange(near_moved)

        def first_base(source_ref, wavelet_ref, receiver_ref, observed_ref, one_ref, inner_out, spots_out):
            weights = plane_weights(rows, columns)

            def particle(p):
                for at, plane in zip(at_plane, inner_laplace(planes_of(one_ref[p], rows), weights)):
                    inner_out[p, at] = plane

            loop(count, particle)
            first_row = lax.axis_index("slab") * depth
            cells = receiver_ref[...]
            row = lax.shift_right_logical(cells, columns.bit_length() - 1) - first_row
            column = cells & (columns - 1)
            hit_row = lax.broadcasted_iota(jnp.int32, (depth, cells.shape[1]), 0) == row
            hit_column = lax.broadcasted_iota(jnp.int32, (columns, cells.shape[1]), 0) == column
            left = jnp.concatenate(
                [jnp.where(hit_row, value, 0.0) for value in (1.0, observed_ref[0:1], observed_ref[1:2])], axis=0
            )
            spots_out[0 : 3 * depth] = lax.dot_general(
                left,
                jnp.where(hit_column, 1.0, 0.0),
                (((1,), (1,)), ((), ())),
                precision=HIGHEST,
                preferred_element_type=F32,
            )
            cell = (lax.broadcasted_iota(jnp.int32, (depth, columns), 0) + first_row) * columns
            cell = cell + lax.broadcasted_iota(jnp.int32, (depth, columns), 1)
            at_source = cell == source_ref[0:1, :]
            spots_out[3 * depth : 4 * depth] = jnp.where(at_source, wavelet_ref[:, 0:1], 0.0)
            spots_out[4 * depth : 5 * depth] = jnp.where(at_source, wavelet_ref[:, 1:2], 0.0)

        one_inner, spots = call(
            first_base,
            [stack, (5 * depth, columns)],
            jnp.broadcast_to(sources[:, None], (rows, columns)),
            *small,
            wave_one,
        )

        def spot(spots_ref, kind, z):
            return spots_ref[kind * depth + z * rows : kind * depth + (z + 1) * rows]

        def first(
            spots_ref, first, second, inner_ref, one_ref, zero_ref, squared_ref, lap_out, wave_out
        ):
            masks = side_masks(rows, columns, flip=True)

            def particle(p):
                below, above = sides(masks, first, second, rows, p)
                before = zero_ref[p].astype(F32)
                for z, at in enumerate(at_plane):
                    lap = inner_ref[p, at] + outer_laplace(below, above, z, layers)
                    lap_out[p, at] = lap
                    moved = squared_ref[p, at] * lap + spot(spots_ref, 3, z)
                    wave_out[p, at] = 2.0 * one_ref[p, at] - before[at] + moved

            loop(count, particle)

        lap_one, wave_two = call(
            first, [stack] * 2, spots, one_first, one_second, one_inner, wave_one, zero, squared
        )
        two_first, two_second = exchange(wave_two)
        others = [from_dom(models, k) for k in range(1, doms)]

        def second_base(first, second, moved_ref, near_ref, far_ref, two_ref, base_out, inner_out):
            weights = plane_weights(rows, columns)
            masks = side_masks(rows, columns)

            def waves(p):
                for at, plane in zip(at_plane, inner_laplace(planes_of(two_ref[p], rows), weights)):
                    inner_out[p, at] = plane

            def adjoints(p):
                below, above = sides(masks, first, second, rows, p)
                later = 2.0 * near_ref[p].astype(F32) - far_ref[p].astype(F32)
                for z, plane in enumerate(inner_laplace(planes_of(moved_ref[p], rows), weights)):
                    at = at_plane[z]
                    base_out[p, at] = later[at] + plane + outer_laplace(below, above, z, layers)

            loop(count, waves)
            loop(count, adjoints)

        base, two_inner = call(
            second_base, [stack] * 2, near_first, near_second, near_moved, near, far, wave_two
        )

        def second(
            spots_ref,
            first,
            second,
            inner_ref,
            one_ref,
            two_ref,
            squared_ref,
            base_ref,
            lap_out,
            three_out,
            moved_out,
        ):
            masks = side_masks(rows, columns)

            def particle(p):
                below, above = sides(masks, first, second, rows, p)
                for z, at in enumerate(at_plane):
                    lap = inner_ref[p, at] + outer_laplace(below, above, z, layers)
                    lap_out[p, at] = lap
                    moved = squared_ref[p, at] * lap + spot(spots_ref, 4, z)
                    wave_three = 2.0 * two_ref[p, at] - one_ref[p, at] + moved
                    three = base_ref[p, at] - (spot(spots_ref, 0, z) * wave_three - spot(spots_ref, 2, z))
                    three_out[p, at] = three
                    moved_out[p, at] = squared_ref[p, at] * three

            loop(count, particle)

        lap_two, three, three_moved = call(
            second,
            [stack] * 3,
            spots,
            two_first,
            two_second,
            two_inner,
            wave_one,
            wave_two,
            squared,
            base,
        )
        three_first, three_second = exchange(three_moved)

        wide = total * rows

        def gram(*refs):
            *parts, out_ref = refs
            side = jnp.concatenate(
                [
                    jnp.concatenate([part[:, at].reshape(count * rows, columns) for part in parts], axis=0)
                    for at in at_plane
                ],
                axis=1,
            )
            same = lax.dot_general(
                side, side, (((1,), (1,)), ((), ())), precision=HIGHEST, preferred_element_type=F32
            )
            r = lax.broadcasted_iota(jnp.int32, (wide, wide), 0)
            c = lax.broadcasted_iota(jnp.int32, (wide, wide), 1)
            same = jnp.where(r % rows == c % rows, same, 0.0)
            same = jnp.sum(same.reshape(total, rows, wide), axis=1)
            step = 1
            while step < rows:
                same = same + pltpu.roll(same, wide - step, 1)
                step *= 2
            first_of = lax.broadcasted_iota(jnp.int32, (total, wide), 1) % rows == 0
            out_ref[...] = jnp.where(first_of, same, 0.0)

        (gram_one,) = call(gram, [(total, wide)], models, *others, flops=LONG)
        if not halving:
            gram_one = lax.psum(gram_one, "slab")
        gram_pair = from_slab(gram_one, 1)

        def third_base(spots_ref, moved_ref, three_ref, near_ref, two_ref, lap_one_ref, lap_two_ref, out_ref):
            weights = plane_weights(rows, columns)

            def particle(p):
                before = near_ref[p].astype(F32)
                for z, lap in enumerate(inner_laplace(planes_of(moved_ref[p], rows), weights)):
                    at = at_plane[z]
                    three = three_ref[p, at]
                    injected = spot(spots_ref, 0, z) * two_ref[p, at] - spot(spots_ref, 1, z)
                    two = 2.0 * three - before[at] + lap - injected
                    out_ref[p, at] = two * lap_one_ref[p, at] + three * lap_two_ref[p, at]

            loop(count, particle)

        (inner_correlation,) = call(
            third_base,
            [stack],
            spots,
            three_moved,
            three,
            near,
            wave_two,
            lap_one,
            lap_two,
        )

        def third(first, second, inner_ref, lap_one_ref, squared_ref, models_ref, out_ref):
            masks = side_masks(rows, columns)

            def particle(p):
                below, above = sides(masks, first, second, rows, p)
                for z, at in enumerate(at_plane):
                    full = inner_ref[p, at] + outer_laplace(below, above, z, layers) * lap_one_ref[p, at]
                    score = DATA_WEIGHT * squared_ref[p, at] * full
                    out_ref[p, at] = score - 0.5 * (PRIOR_WEIGHT + REPEL_WEIGHT) * models_ref[p, at]

            loop(count, particle)

        (pull,) = call(
            third,
            [stack],
            three_first,
            three_second,
            inner_correlation,
            lap_one,
            squared,
            models,
        )
        far_pulls = [from_dom(pull, k) for k in range(1, doms)]
        pull_pair = other_shot(pull)

        far_pairs = [other_shot(block) for block in far_pulls]

        def plus(first_ref, second_ref, out_ref):
            out_ref[...] = first_ref[...] + second_ref[...]

        step = 2
        while halving and step < slabs:
            (gram_one,) = call(plus, [(total, wide)], gram_one, gram_pair, flops=LONG)
            gram_pair = from_slab(gram_one, step)
            step *= 2
        (gram_one,) = call(plus, [(total, wide)], gram_one, gram_pair, flops=LONG)

        def spread(gram_ref, out_ref):
            value = gram_ref[...]
            r = lax.broadcasted_iota(jnp.int32, (total, wide), 0)
            c = lax.broadcasted_iota(jnp.int32, (total, wide), 1)
            diagonal = jnp.where(r * rows == c, value, 0.0)
            distance = jnp.sum(diagonal, axis=1, keepdims=True) + jnp.sum(diagonal, axis=0, keepdims=True) - 2.0 * value
            distance = jnp.where(c % rows == 0, distance, 0.0)
            width = jnp.sum(jnp.sum(distance, axis=1, keepdims=True), axis=0, keepdims=True) / (
                total * (total - 1) * math.log(total)
            )
            kernel = jnp.where(c % rows == 0, jnp.exp(-distance / width), 0.0)
            kernel = kernel / jnp.sum(kernel, axis=1, keepdims=True)
            for j in range(total):
                out_ref[j] = jnp.broadcast_to(kernel[:count, j * rows : j * rows + 1], (count, columns))

        (spread_kernel,) = call(spread, [(total, count, columns)], gram_one, flops=LONG)

        def weigh(kernel_ref, start, pulled, values):
            for j in range(len(values)):
                for i in range(count):
                    pulled[i] = pulled[i] + kernel_ref[start + j, i : i + 1] * values[j]
            return pulled

        def last_base(kernel_ref, pull_ref, pair_ref, models_ref, out_ref):
            for at in at_plane:
                pulled = [REPEL_WEIGHT * models_ref[i, at] for i in range(count)]
                pulled = weigh(kernel_ref, 0, pulled, [pull_ref[j, at] + pair_ref[j, at] for j in range(count)])
                for i in range(count):
                    out_ref[i, at] = pulled[i]

        (update_base,) = call(last_base, [stack], spread_kernel, pull, pull_pair, models)

        def last(kernel_ref, base_ref, *refs):
            *pulls, out_ref = refs
            for at in at_plane:
                pulled = [base_ref[i, at] for i in range(count)]
                for k in range(1, doms):
                    here, there = pulls[k - 1], pulls[doms - 1 + k - 1]
                    pulled = weigh(kernel_ref, k * count, pulled, [here[j, at] + there[j, at] for j in range(count)])
                for i in range(count):
                    out_ref[i, at] = pulled[i]

        (update,) = call(last, [stack], spread_kernel, update_base, *far_pulls, *far_pairs)
        return update.reshape(particles.shape)

    placed = (
        P(("grp", "dom"), "slab", None, None),
        P(("grp", "slab"), None, None),
        P(("grp", "dom"), "shot", "slab", None, None),
        P(("grp", "dom"), "shot", "slab", None, None),
        P(("grp", "dom"), "shot", "slab", None, None),
        P(("grp", "dom"), "shot", "slab", None, None),
        P(("grp", "shot")),
        P(("grp", "shot"), None),
        P(("grp", "shot"), None),
        P(("grp", "shot"), None, None),
    )
    return jax.shard_map(
        local,
        mesh=mesh,
        in_specs=placed,
        out_specs=P(("grp", "dom"), "slab", None, None),
        check_vma=False,
    )
```
